256 devices in a mesh: rows: 64 (over y_lo, z, x), rep: 4 (over y_hi, core).
Axes of the slice: x: 4, y: 4 (y_hi: 2, y_lo: 2; y = y_hi * 2 + y_lo), z: 8, core: 2. Of those that a mesh axis runs over, the one named last changes fastest.
Arguments:
- features: bfloat16 [131072, 128], P('rows'), may hold values from -6 to 6
- adjacency: bfloat16 [64, 4, 2, 40, 256, 256], P('rows', 'rep'), may hold values from -0.0625 to 0.0625
- tile_coords: int32 [64, 4, 2, 2, 40], P('rows', 'rep'), may hold values from 0 to 7, as said below
- tile_counts: int32 [64, 4, 2], P('rows', 'rep'), may hold values from 1 to 40, as said below
- weight: bfloat16 [128, 256], replicated, may hold values from -0.5 to 0.5
- bias: float32 [256], replicated, may hold values from -3 to 3
- cotangent: bfloat16 [131072, 256], P(('rows', 'rep'))
Outputs:
- hidden: bfloat16 [131072, 256], P(('rows', 'rep'))
- grad_inputs: bfloat16 [4, 2, 2048, 128], P('rep', None, 'rows')
- grad_weight: float32 [128, 256], replicated
- grad_bias: float32 [256], replicated
The draws below stay inside these ranges and needn't reach their ends.
Inputs may be any that keep to these rules, and one draw needn't show every extreme that they name: tile_coords[i, g, s, 0, t] and tile_coords[i, g, s, 1, t] are the tile row in row block i and the tile column in column block c(g, s) of slot t; the 40 positions of one row block, group and section are distinct; slots at or past the count hold no tile. `tile_counts`: for every replica group and section some row block has exactly 40 live slots.
All inputs are finite; a program needn't handle non-finite values.
Results may differ from the reference program's by a relative error of at most 0.0059.
Values may be sent and summed in bfloat16 or wider, within the bound.
A program may use at most 128 MiB of HBM per device.

```python
import math
import jax
import jax.numpy as jnp
from jax import lax

F_IN = 128
HID = 256
TILE = 256
SECTIONS = 2
BLK = 2048
MAXT = 40
NODES = 131072
N_ROWS = 64
N_REP = 4


def draw_tile_coords(key, part):
    key = jax.random.fold_in(key, 7)
    tiles_side = BLK // TILE
    total_lists = N_ROWS * N_REP * SECTIONS
    keys = jax.random.split(key, total_lists)
    orders = jax.vmap(lambda seed_key: jax.random.permutation(seed_key, tiles_side * tiles_side)[:MAXT])(keys)
    orders = orders.reshape(N_ROWS, N_REP, SECTIONS, MAXT)
    tile_rows = orders // tiles_side
    tile_cols = orders % tiles_side
    return jnp.stack([tile_rows, tile_cols], axis=3).astype(jnp.int32)


def draw_tile_counts(key, part):
    key = jax.random.fold_in(key, 5)
    first_key, second_key, third_key = jax.random.split(key, 3)
    first = jax.random.randint(first_key, (N_ROWS, N_REP, SECTIONS), 1, MAXT + 1)
    second = jax.random.randint(second_key, (N_ROWS, N_REP, SECTIONS), 1, MAXT + 1)
    counts = jnp.minimum(first, second)
    chosen_rows = jax.random.randint(third_key, (N_REP, SECTIONS), 0, N_ROWS)
    forced = jnp.arange(N_ROWS)[:, None, None] == chosen_rows[None, :, :]
    return jnp.where(forced, MAXT, counts).astype(jnp.int32)


def draw_cotangent(key, part):
    key = jax.random.fold_in(key, 11)
    base_key = jax.random.fold_in(key, 0)
    position = jnp.arange(NODES, dtype=jnp.float32) / NODES
    base = jax.random.normal(base_key, (NODES, HID), jnp.float32)
    values = base * (0.5 + position)[:, None]
    return values.astype(jnp.bfloat16)


def levels(stream_key, extent, cuts, least, largest):
    factor_of, own = 1.0, jax.random.fold_in(stream_key, 6)
    for dim, blocks in cuts:
        heights = jnp.exp(jax.random.uniform(jax.random.fold_in(own, dim), (blocks,), jnp.float32, least / len(cuts), largest / len(cuts)))
        factor_of = factor_of * jnp.repeat(heights, extent[dim] // blocks).reshape([-1 if axis == dim else 1 for axis in range(len(extent))])
    return factor_of


def scatter_about(stream_key, dims, deviation, bound, shards=(), kind=jnp.bfloat16):
    values = jax.random.normal(stream_key, dims, jnp.float32) * deviation
    if len(shards) > 0:
        values = levels(stream_key, dims, shards, -0.22, 0.18) * values
    return jnp.clip(values, min=-bound, max=bound).astype(kind)


def setup_inputs(seed: int = 0) -> dict:
    streams_of = jax.random.split(jax.random.key(seed), 8)
    return {
        "features": scatter_about(streams_of[0], (NODES, F_IN), 1.0, 6.0, ((0, 64),)),
        "adjacency": scatter_about(streams_of[1], (N_ROWS, N_REP, SECTIONS, MAXT, TILE, TILE), (TILE * MAXT) ** -0.5, 0.0625, ((0, 64), (1, 4))),
        "tile_coords": draw_tile_coords(jax.random.fold_in(streams_of[7], 71), 0),
        "tile_counts": draw_tile_counts(jax.random.fold_in(streams_of[7], 71), 0),
        "weight": scatter_about(streams_of[4], (F_IN, HID), F_IN ** -0.5, 0.5),
        "bias": scatter_about(streams_of[5], (HID,), 0.5, 3.0, (), jnp.float32),
        "cotangent": draw_cotangent(jax.random.fold_in(streams_of[7], 71), 0),
    }


def pick_matrix(target, live_count, tiles_side, slot_count):
    slot_index = jnp.arange(slot_count, dtype=jnp.int32)
    is_live = slot_index[None, None, :] < live_count[:, :, None]
    same = jnp.arange(tiles_side, dtype=jnp.int32)[None, None, :, None] == target[:, :, None, :]
    return (same & is_live[:, :, None, :]).astype(jnp.float32)

def gelu_tanh(value):
    return jax.nn.gelu(value, approximate=True)

def reference(features, adjacency, tile_coords, tile_counts, weight, bias, cotangent):
    tiles_side = BLK // TILE
    spacing = N_ROWS // (N_REP * SECTIONS)
    owners = ((jnp.arange(N_REP, dtype=jnp.int32)[:, None] * SECTIONS + jnp.arange(SECTIONS, dtype=jnp.int32)[None, :]) * spacing).astype(jnp.int32)
    feat_tiles = features.reshape(N_ROWS, tiles_side, TILE, F_IN)
    highest = lax.Precision.HIGHEST

    def forward_block(block_index):
        tile_values = adjacency[block_index].astype(jnp.float32)
        tile_place = tile_coords[block_index]
        chosen = feat_tiles[owners[:, :, None], tile_place[:, :, 1]].astype(jnp.float32)
        products = jnp.einsum('abtij,abtjf->abtif', tile_values, chosen, precision=highest)
        placed = pick_matrix(tile_place[:, :, 0], tile_counts[block_index], tiles_side, MAXT)
        summed = jnp.einsum('abpt,abtif->pif', placed, products, precision=highest)
        return summed.reshape(BLK, F_IN)
    aggregate = lax.map(forward_block, jnp.arange(N_ROWS, dtype=jnp.int32)).reshape(NODES, F_IN)
    aggregate_bf = aggregate.astype(jnp.bfloat16)
    preact = jnp.dot(aggregate_bf, weight, preferred_element_type=jnp.float32) + bias
    activated, pullback = jax.vjp(gelu_tanh, preact)
    hidden = activated.astype(jnp.bfloat16)
    grad_pre = pullback(cotangent.astype(jnp.float32))[0]
    grad_pre_bf = grad_pre.astype(jnp.bfloat16)
    scale_factor = 1.0 / math.sqrt(NODES)
    grad_weight = lax.dot_general(aggregate_bf, grad_pre_bf, (((0,), (0,)), ((), ())), preferred_element_type=jnp.float32) * scale_factor
    grad_bias = lax.optimization_barrier(jnp.sum(grad_pre, axis=0)) * scale_factor
    grad_rows = lax.dot_general(grad_pre_bf, weight, (((1,), (1,)), ((), ())), preferred_element_type=jnp.float32).astype(jnp.bfloat16)
    grad_tiles = grad_rows.reshape(N_ROWS, tiles_side, TILE, F_IN)

    def backward_block(running, block_index):
        tile_values = adjacency[block_index].astype(jnp.float32)
        tile_place = tile_coords[block_index]
        chosen = grad_tiles[block_index][tile_place[:, :, 0]].astype(jnp.float32)
        products = jnp.einsum('abtji,abtjf->abtif', tile_values, chosen, precision=highest)
        placed = pick_matrix(tile_place[:, :, 1], tile_counts[block_index], tiles_side, MAXT)
        summed = jnp.einsum('abpt,abtif->abpif', placed, products, precision=highest)
        return (running + summed, None)
    start = jnp.zeros((N_REP, SECTIONS, tiles_side, TILE, F_IN), jnp.float32)
    total = lax.scan(backward_block, start, jnp.arange(N_ROWS, dtype=jnp.int32))[0]
    grad_inputs = total.reshape(N_REP, SECTIONS, BLK, F_IN).astype(jnp.bfloat16)
    return (hidden, grad_inputs, grad_weight, grad_bias)
```

```python
import functools
import math

import jax
import jax.numpy as jnp
from jax import lax
from jax.experimental import pallas as pl
from jax.experimental.pallas import tpu as pltpu
from jax.sharding import PartitionSpec as P

MESH = pl.DeviceIdType.MESH
F32 = jnp.float32
BF16 = jnp.bfloat16
SLOTS = 80
XY_ORDER = (1, 3, 4, 5, 7, 2, 6)


def mm(a, b):
    return lax.dot_general(a, b, (((1,), (0,)), ((), ())), preferred_element_type=F32)


def mm_nt(a, b):
    return lax.dot_general(a, b, (((1,), (1,)), ((), ())), preferred_element_type=F32)


def mm_tn(a, b):
    return lax.dot_general(a, b, (((0,), (0,)), ((), ())), preferred_element_type=F32)


def arrived(ref, sem):
    pltpu.make_async_copy(ref, ref, sem).wait()


def kernel(
    scale,
    feat_hbm, adj_hbm, tab, w_ref, b_ref, cot_ref,
    hid_ref, gin_ref, gw_ref, gb_ref,
    adj, feat, acc, ps, pr, rt, acct, xs, xr, zs, zr, wa_s, wa, wb, wc,
    adj_sem, s1, s2, s3, r12, r3, ps_s, ps_r, rt_s, rt_r,
    wa_ss, wa_rs, wb_ss, wb_rs, wc_ss, wc_rs, xs_s, xs_r, zs_s, zs_r,
):
    row = lax.axis_index("rows")
    rep = lax.axis_index("rep")
    x = lax.rem(row, 4)
    z = lax.rem(lax.div(row, 4), 8)
    yl = lax.div(row, 32)
    yh = lax.div(rep, 2)
    core = lax.rem(rep, 2)

    def device(x, yl, z, yh, core):
        return (yl * 32 + z * 4 + x, yh * 2 + core)

    def xy_at(k, sign=1):
        return lax.rem(x + sign * (k % 4) + 4, 4), lax.rem(yl + k // 4, 2)

    def xy_peer(k):
        px, pyl = xy_at(k)
        return device(px, pyl, z, yh, core)

    def z_peer(k):
        return device(x, yl, lax.rem(z + k, 8), yh, core)

    def rep_peer(k):
        return device(x, yl, z, lax.rem(yh + k // 2, 2), lax.rem(core + k % 2, 2))

    a_pos = z * 2 + core
    b_pos = (yh * 2 + yl) * 4 + x

    def a_at(k):
        return lax.rem(a_pos + k, 16)

    def a_peer(k):
        pos = a_at(k)
        return device(x, yl, lax.div(pos, 2), yh, lax.rem(pos, 2))

    def b_peer(k):
        pos = lax.rem(b_pos + k, 16)
        py = lax.div(pos, 4)
        return device(lax.rem(pos, 4), lax.rem(py, 2), z, lax.div(py, 2), core)

    def send(src, dst, send_sem, recv_sem, peer):
        return pltpu.make_async_remote_copy(
            src_ref=src, dst_ref=dst, send_sem=send_sem, recv_sem=recv_sem,
            device_id=peer, device_id_type=MESH,
        )

    part = SLOTS // 4
    for i in range(4):
        pltpu.make_async_copy(
            adj_hbm.at[pl.ds(i * part, part)], adj.at[pl.ds(i * part, part)], adj_sem.at[i]
        ).start()

    barrier = pltpu.get_barrier_semaphore()
    greet = [xy_peer(k) for k in range(1, 8)]
    greet += [rep_peer(k) for k in range(1, 4)]
    greet += [a_peer(k) for k in range(1, 16)]
    for k in range(8):
        px, pyl = xy_at(k)
        if k > 0:
            greet.append(device(px, pyl, z, lax.rem(yh + 1, 2), core))
    for peer in greet:
        pl.semaphore_signal(barrier, inc=1, device_id=peer, device_id_type=MESH)
    pl.semaphore_wait(barrier, len(greet))

    my_j = yl * 4 + x
    is_root = [row == (rep * 2 + s) * 8 for s in range(2)]
    in_plane = [z == core * 4 + s * 2 for s in range(2)]

    def root_copy(s, k):
        px, pyl = xy_at(k)
        j = pyl * 4 + px
        return send(
            feat_hbm.at[pl.ds(pl.multiple_of(j * 256, 256), 256)], feat.at[s, j],
            s1.at[s, k], r12.at[s], device(px, pyl, z, yh, core),
        )

    def plane_copy(s, k):
        return send(feat.at[s, my_j], feat.at[s, my_j], s2.at[s, k], r12.at[s], z_peer(k))

    def side_copy(s, k):
        return send(feat.at[s, my_j], feat.at[s, my_j], s3.at[s, k], r3.at[s, k], xy_peer(k))

    for s in range(2):
        @pl.when(is_root[s])
        def _():
            for k in XY_ORDER:
                root_copy(s, k).start()
            pltpu.make_async_copy(
                feat_hbm.at[pl.ds(pl.multiple_of(my_j * 256, 256), 256)], feat.at[s, my_j], r12.at[s]
            ).start()

    acc[...] = jnp.zeros_like(acc)
    adj[SLOTS] = jnp.zeros((256, 256), BF16)

    for s in range(2):
        arrived(feat.at[s, my_j], r12.at[s])

        @pl.when(in_plane[s])
        def _():
            for k in (4, 3, 5, 2, 6, 1, 7):
                plane_copy(s, k).start()

        for k in XY_ORDER:
            side_copy(s, k).start()

    for i in range(4):
        view = adj.at[pl.ds(i * part, part)]
        arrived(view, adj_sem.at[i])

    def forward(i, carry):
        s = lax.div(i, 8)
        k = lax.rem(i, 8)
        fx = lax.rem(x - lax.rem(k, 4) + 4, 4)
        fyl = lax.rem(yl + lax.div(k, 4), 2)
        j = fyl * 4 + fx

        @pl.when(k > 0)
        def _():
            arrived(feat.at[s, j], r3.at[s, k])

        column = feat[s, j]
        for p in range(8):
            acc[p] += mm(adj[tab[s * 64 + p * 8 + j]], column)
        return carry

    lax.fori_loop(0, 16, forward, 0)

    def part_copy(k):
        return send(ps.at[k], pr.at[k], ps_s.at[k], ps_r.at[k], rep_peer(k))

    for k in (3, 2, 1):
        target = lax.rem(yh + k // 2, 2) * 2 + lax.rem(core + k % 2, 2)
        for h in range(2):
            ps[k, pl.ds(h * 256, 256)] = acc[target * 2 + h].astype(BF16)
        part_copy(k).start()
    for k in (1, 2, 3):
        arrived(pr.at[k], ps_r.at[k])

    c0 = math.sqrt(2.0 / math.pi)
    weight = w_ref[...]

    def epilogue(h, carry):
        wsum, bsum = carry
        rows = pl.ds(pl.multiple_of(h * 256, 256), 256)
        total = acc[rep * 2 + h] + pr[1, rows].astype(F32)
        total += pr[2, rows].astype(F32)
        total += pr[3, rows].astype(F32)
        agg = total.astype(BF16)
        v = mm(agg, weight) + b_ref[...]
        v2 = v * v
        t = jnp.tanh(c0 * (v + 0.044715 * (v2 * v)))
        half = 0.5 * (1.0 + t)
        hid_ref[rows] = (v * half).astype(BF16)
        slope = half + 0.5 * v * (1.0 - t * t) * (c0 * (1.0 + 0.134145 * v2))
        grad = cot_ref[rows].astype(F32) * slope
        grad_bf = grad.astype(BF16)
        rt[rep, :, rows] = mm_nt(weight, grad_bf).astype(BF16)
        wsum = wsum + mm_tn(agg, grad_bf)
        bsum = bsum + jnp.sum(grad.reshape(32, 8, 256), axis=0)
        return wsum, bsum

    carry = (jnp.zeros((128, 256), F32), jnp.zeros((8, 256), F32))
    for h in range(2):
        carry = epilogue(h, carry)
    wsum, bsum = carry

    def rows_copy(k):
        return send(rt.at[rep], rt.at[rep], rt_s.at[k], rt_r.at[k], rep_peer(k))

    for k in (3, 2, 1):
        rows_copy(k).start()

    for j in range(16):
        wa_s[j, pl.ds(0, 8)] = wsum[j * 8 : j * 8 + 8]
        wa_s[j, pl.ds(8, 8)] = bsum

    def wa_copy(k):
        return send(wa_s.at[a_at(k)], wa.at[a_pos], wa_ss.at[k], wa_rs.at[k], a_peer(k))

    for k in range(1, 16):
        wa_copy(k).start()
    wa[a_pos] = wa_s[a_pos]

    def quarter_of(k):
        return lax.rem(yh + k // 2, 2) * 2 + lax.rem(core + k % 2, 2)

    def back_terms(s, q, quarter):
        left = rt[quarter]
        out = mm(left[:, :256], adj[tab[s * 64 + quarter * 16 + q]])
        return out + mm(left[:, 256:], adj[tab[s * 64 + quarter * 16 + 8 + q]])

    def back_own(i, carry):
        s, q = lax.div(i, 8), lax.rem(i, 8)
        acct[s, q] = back_terms(s, q, quarter_of(0))
        return carry

    lax.fori_loop(0, 16, back_own, 0)
    arrived(rt.at[quarter_of(1)], rt_r.at[1])

    def back_core(i, carry):
        s, q = lax.div(i, 8), lax.rem(i, 8)
        acct[s, q] += back_terms(s, q, quarter_of(1))
        return carry

    lax.fori_loop(0, 16, back_core, 0)
    for k in (2, 3):
        arrived(rt.at[quarter_of(k)], rt_r.at[k])

    def xs_copy(s, k):
        px, pyl = xy_at(k)
        return send(xs.at[s, pyl * 4 + px], xr.at[s, k], xs_s.at[s, k], xs_r.at[s, k], xy_peer(k))

    for hk in (1, 0):
        half = lax.rem(yl + hk, 2)
        for s in range(2):
            def back_rest(zz, carry):
                q = half * 4 + zz
                total = acct[s, q] + back_terms(s, q, quarter_of(2))
                total += back_terms(s, q, quarter_of(3))
                out = total.T.astype(BF16)
                for zl in range(2):
                    for px in range(4):
                        at = zl * 128 + px * 32
                        xs[s, half * 4 + px, zz * 2 + zl] = out[at : at + 32]
                return carry

            lax.fori_loop(0, 4, back_rest, 0)
            for k in (1, 3, 2) if hk == 0 else (4, 5, 7, 6):
                xs_copy(s, k).start()

    for k in range(1, 16):
        arrived(wa.at[lax.rem(a_pos - k + 16, 16)], wa_rs.at[k])
    total = wa[0]
    for j in range(1, 16):
        total = total + wa[j]
    wb[b_pos] = total

    def wb_copy(k):
        return send(wb.at[b_pos], wb.at[b_pos], wb_ss.at[k], wb_rs.at[k], b_peer(k))

    for k in range(1, 16):
        wb_copy(k).start()

    def zs_copy(s, k):
        return send(zs.at[s, lax.rem(z + k, 8)], zr.at[s, k], zs_s.at[s, k], zs_r.at[s, k], z_peer(k))

    for s in range(2):
        for k in range(1, 8):
            arrived(xr.at[s, k], xs_r.at[s, k])
        for zz in range(8):
            total = xs[s, my_j, zz].astype(F32)
            for k in range(1, 8):
                total += xr[s, k, zz].astype(F32)
            zs[s, zz] = total.astype(BF16)
        for k in (4, 3, 5, 2, 6, 1, 7):
            zs_copy(s, k).start()

    for k in range(1, 16):
        arrived(wb.at[lax.rem(b_pos - k + 16, 16)], wb_rs.at[k])
    total = wb[0]
    for j in range(1, 16):
        total = total + wb[j]
    wc[a_pos] = total[:8] * scale
    gb_ref[...] = jnp.sum(total[8:], axis=0, keepdims=True) * scale

    def wc_copy(k):
        return send(wc.at[a_pos], wc.at[a_pos], wc_ss.at[k], wc_rs.at[k], a_peer(k))

    for k in range(1, 16):
        wc_copy(k).start()

    for s in range(2):
        total = zs[s, z].astype(F32)
        for k in range(1, 8):
            arrived(zr.at[s, k], zs_r.at[s, k])
            total += zr[s, k].astype(F32)
        gin_ref[s] = total.astype(BF16)

    for k in range(1, 16):
        arrived(wc.at[lax.rem(a_pos - k + 16, 16)], wc_rs.at[k])
    gw_ref[...] = wc[...]

    for s in range(2):
        @pl.when(is_root[s])
        def _():
            for k in range(1, 8):
                root_copy(s, k).wait_send()

        @pl.when(in_plane[s])
        def _():
            for k in range(1, 8):
                plane_copy(s, k).wait_send()

        for k in range(1, 8):
            side_copy(s, k).wait_send()
            xs_copy(s, k).wait_send()
            zs_copy(s, k).wait_send()
    for k in range(1, 4):
        part_copy(k).wait_send()
        rows_copy(k).wait_send()
    for k in range(1, 16):
        wa_copy(k).wait_send()
        wb_copy(k).wait_send()
        wc_copy(k).wait_send()


def layer(features, adjacency, table, weight, bias, cotangent, scale):
    vmem = pl.BlockSpec(memory_space=pltpu.VMEM)
    hbm = pl.BlockSpec(memory_space=pl.ANY)
    sems = [
        (4,), (2, 8), (2, 8), (2, 8), (2,), (2, 8), (4,), (4,), (4,), (4,),
        (16,), (16,), (16,), (16,), (16,), (16,), (2, 8), (2, 8), (2, 8), (2, 8),
    ]
    return pl.pallas_call(
        functools.partial(kernel, scale),
        name="layer",
        out_shape=(
            jax.ShapeDtypeStruct((512, 256), BF16),
            jax.ShapeDtypeStruct((2, 32, 128), BF16),
            jax.ShapeDtypeStruct((16, 8, 256), F32),
            jax.ShapeDtypeStruct((1, 256), F32),
        ),
        in_specs=[hbm, hbm, pl.BlockSpec(memory_space=pltpu.SMEM), vmem, vmem, vmem],
        out_specs=(vmem, vmem, vmem, vmem),
        scratch_shapes=[
            pltpu.VMEM((SLOTS + 1, 256, 256), BF16),
            pltpu.VMEM((2, 8, 256, 128), BF16),
            pltpu.VMEM((8, 256, 128), F32),
            pltpu.VMEM((4, 512, 128), BF16),
            pltpu.VMEM((4, 512, 128), BF16),
            pltpu.VMEM((4, 128, 512), BF16),
            pltpu.VMEM((2, 8, 128, 256), F32),
            pltpu.VMEM((2, 8, 8, 32, 128), BF16),
            pltpu.VMEM((2, 8, 8, 32, 128), BF16),
            pltpu.VMEM((2, 8, 32, 128), BF16),
            pltpu.VMEM((2, 8, 32, 128), BF16),
            pltpu.VMEM((16, 16, 256), F32),
            pltpu.VMEM((16, 16, 256), F32),
            pltpu.VMEM((16, 16, 256), F32),
            pltpu.VMEM((16, 8, 256), F32),
        ]
        + [pltpu.SemaphoreType.DMA(shape) for shape in sems],
        compiler_params=pltpu.CompilerParams(
            collective_id=1, has_side_effects=True, vmem_limit_bytes=40 * 2**20
        ),
    )(features, adjacency, table, weight, bias, cotangent)


def shards(features, adjacency, tile_coords, tile_counts, weight, bias, cotangent):
    rows_count = lax.axis_size("rows")
    scale = 1.0 / math.sqrt(features.shape[0] * rows_count)
    coords = tile_coords[0, 0]
    counts = tile_counts[0, 0]
    slot = jnp.arange(40, dtype=jnp.int32)
    place = jnp.where(slot[None, :] < counts[:, None], coords[:, 0] * 8 + coords[:, 1], -1)
    hit = place[:, None, :] == jnp.arange(64, dtype=jnp.int32)[None, :, None]
    number = slot[None, None, :] + 40 * jnp.arange(2, dtype=jnp.int32)[:, None, None] - SLOTS
    table = SLOTS + jnp.sum(jnp.where(hit, number, 0), axis=2)
    hidden, grad_inputs, grad_weight, grad_bias = layer(
        features,
        adjacency.reshape(SLOTS, 256, 256),
        table.reshape(128),
        weight,
        bias.reshape(1, 256),
        cotangent,
        scale,
    )
    return hidden, grad_inputs[None], grad_weight.reshape(128, 256), grad_bias.reshape(256)


def solution(mesh):
    return jax.shard_map(
        shards,
        mesh=mesh,
        in_specs=(
            P("rows", None),
            P("rows", "rep", None, None, None, None),
            P("rows", "rep", None, None, None),
            P("rows", "rep", None),
            P(),
            P(),
            P(("rows", "rep"), None),
        ),
        out_specs=(P(("rows", "rep"), None), P("rep", None, "rows", None), P(), P()),
        check_vma=False,
    )
```

```python
import functools
import math

import jax
import jax.numpy as jnp
from jax import lax
from jax.experimental import pallas as pl
from jax.experimental.pallas import tpu as pltpu
from jax.sharding import PartitionSpec as P

MESH = pl.DeviceIdType.MESH
F32 = jnp.float32
BF16 = jnp.bfloat16
SLOTS = 80
VMEM_BYTES = 62 * 2**20
XY_ORDER = (1, 3, 4, 5, 7, 2, 6)


def mm(a, b):
    return lax.dot_general(a, b, (((1,), (0,)), ((), ())), preferred_element_type=F32)


def mm_nt(a, b):
    return lax.dot_general(a, b, (((1,), (1,)), ((), ())), preferred_element_type=F32)


def mm_tn(a, b):
    return lax.dot_general(a, b, (((0,), (0,)), ((), ())), preferred_element_type=F32)


def arrived(ref, sem):
    pltpu.make_async_copy(ref, ref, sem).wait()


def kernel(
    scale,
    feat_hbm, adj_hbm, tab, w_hbm, b_hbm, cot_hbm,
    hid_hbm, gin_hbm, gw_hbm, gb_hbm,
    adj, feat, acc, pf, ps, pr, rt, acct, xs, xr, zs, zr,
    w_ref, b_ref, cot_ref, hid_ref, gin_ref, gb_ref, wa_s, wa, wb, wc, ba_s, ba, bb, bc,
    adj_sem, in_sem, out_sem, s1, s2, s3, r12, r3, ps_s, ps_r, rt_s, rt_r,
    wa_ss, wa_rs, wb_ss, wb_rs, wc_ss, wc_rs,
    ba_ss, ba_rs, bb_ss, bb_rs, bc_ss, bc_rs, xs_s, xs_r, zs_s, zs_r,
):
    row = lax.axis_index("rows")
    rep = lax.axis_index("rep")
    x = lax.rem(row, 4)
    z = lax.rem(lax.div(row, 4), 8)
    yl = lax.div(row, 32)
    yh = lax.div(rep, 2)
    core = lax.rem(rep, 2)

    def device(x, yl, z, yh, core):
        return (yl * 32 + z * 4 + x, yh * 2 + core)

    def xy_at(k, sign=1):
        return lax.rem(x + sign * (k % 4) + 4, 4), lax.rem(yl + k // 4, 2)

    def xy_peer(k):
        px, pyl = xy_at(k)
        return device(px, pyl, z, yh, core)

    def z_peer(k):
        return device(x, yl, lax.rem(z + k, 8), yh, core)

    def rep_peer(k):
        return device(x, yl, z, lax.rem(yh + k // 2, 2), lax.rem(core + k % 2, 2))

    a_pos = (yh * 2 + yl) * 4 + x
    b_pos = z * 2 + core

    def a_at(k):
        return lax.rem(a_pos + k, 16)

    def a_peer(k):
        pos = a_at(k)
        py = lax.div(pos, 4)
        return device(lax.rem(pos, 4), lax.rem(py, 2), z, lax.div(py, 2), core)

    def b_peer(k):
        pos = lax.rem(b_pos + k, 16)
        return device(x, yl, lax.div(pos, 2), yh, lax.rem(pos, 2))

    def send(src, dst, send_sem, recv_sem, peer):
        return pltpu.make_async_remote_copy(
            src_ref=src, dst_ref=dst, send_sem=send_sem, recv_sem=recv_sem,
            device_id=peer, device_id_type=MESH,
        )

    sent = []

    part = SLOTS // 4
    for i in range(4):
        pltpu.make_async_copy(
            adj_hbm.at[pl.ds(i * part, part)], adj.at[pl.ds(i * part, part)], adj_sem.at[i]
        ).start()

    small = [(w_hbm, w_ref), (b_hbm, b_ref), (cot_hbm, cot_ref)]
    for i, (src, dst) in enumerate(small):
        pltpu.make_async_copy(src, dst, in_sem.at[i]).start()

    barrier = pltpu.get_barrier_semaphore()
    greet = [a_peer(k) for k in range(1, 16)]
    greet += [b_peer(k) for k in range(1, 16)]
    greet.append(rep_peer(3))
    for peer in greet:
        pl.semaphore_signal(barrier, inc=1, device_id=peer, device_id_type=MESH)
    pl.semaphore_wait(barrier, len(greet))

    my_j = yl * 4 + x
    is_root = [row == (rep * 2 + s) * 8 for s in range(2)]
    in_plane = [z == core * 4 + s * 2 for s in range(2)]

    def root_copy(s, k):
        px, pyl = xy_at(k)
        j = pyl * 4 + px
        return send(
            feat_hbm.at[pl.ds(pl.multiple_of(j * 256, 256), 256)], feat.at[s, j],
            s1.at[s, k], r12.at[s], device(px, pyl, z, yh, core),
        )

    def plane_copy(s, k):
        return send(feat.at[s, my_j], feat.at[s, my_j], s2.at[s, k], r12.at[s], z_peer(k))

    def side_copy(s, k):
        return send(feat.at[s, my_j], feat.at[s, my_j], s3.at[s, k], r3.at[s, k], xy_peer(k))

    def drain_if(cond, copy, s):
        @pl.when(cond)
        def _():
            for k in range(1, 8):
                copy(s, k).wait_send()

    for s in range(2):
        @pl.when(is_root[s])
        def _():
            for k in XY_ORDER:
                root_copy(s, k).start()
            pltpu.make_async_copy(
                feat_hbm.at[pl.ds(pl.multiple_of(my_j * 256, 256), 256)], feat.at[s, my_j], r12.at[s]
            ).start()

        sent.append(functools.partial(drain_if, is_root[s], root_copy, s))

    acc[...] = jnp.zeros_like(acc)
    adj[SLOTS] = jnp.zeros((256, 256), BF16)

    for s in range(2):
        arrived(feat.at[s, my_j], r12.at[s])

        @pl.when(in_plane[s])
        def _():
            for k in (4, 3, 5, 2, 6, 1, 7):
                plane_copy(s, k).start()

        sent.append(functools.partial(drain_if, in_plane[s], plane_copy, s))

        for k in XY_ORDER:
            side_copy(s, k).start()
            sent.append(side_copy(s, k).wait_send)

    for i, (src, dst) in enumerate(small):
        arrived(dst, in_sem.at[i])
    for i in range(4):
        view = adj.at[pl.ds(i * part, part)]
        arrived(view, adj_sem.at[i])

    def forward(i, carry):
        s = lax.div(i, 8)
        k = lax.rem(i, 8)
        fx = lax.rem(x - lax.rem(k, 4) + 4, 4)
        fyl = lax.rem(yl + lax.div(k, 4), 2)
        j = fyl * 4 + fx

        @pl.when(k > 0)
        def _():
            arrived(feat.at[s, j], r3.at[s, k])

        column = feat[s, j]
        for p in range(8):
            acc[p] += mm(adj[tab[s * 64 + p * 8 + j]], column)
        return carry

    lax.fori_loop(0, 16, forward, 0)

    far_yh, other = lax.rem(yh + 1, 2), lax.rem(core + 1, 2)

    def core_copy(i):
        quarter = (far_yh, yh)[i] * 2 + other
        return send(acc.at[pl.ds(quarter * 2, 2)], pf.at[i], ps_s.at[i], ps_r.at[i], rep_peer(1))

    def far_copy(h):
        return send(ps.at[h], pr.at[h], ps_s.at[2 + h], ps_r.at[2 + h], rep_peer(2))

    for i in range(2):
        core_copy(i).start()
        sent.append(core_copy(i).wait_send)
    arrived(pf.at[0], ps_r.at[0])
    for h in range(2):
        ps[h] = (acc[(far_yh * 2 + core) * 2 + h] + pf[0, h]).astype(BF16)
        far_copy(h).start()
        sent.append(far_copy(h).wait_send)
    arrived(pf.at[1], ps_r.at[1])

    c0 = math.sqrt(2.0 / math.pi)
    weight = w_ref[...]

    def epilogue(h, carry):
        wsum, bsum = carry
        rows = pl.ds(pl.multiple_of(h * 256, 256), 256)
        total = acc[rep * 2 + h] + pf[1, h]
        arrived(pr.at[h], ps_r.at[2 + h])
        total += pr[h].astype(F32)
        agg = total.astype(BF16)
        v = mm(agg, weight) + b_ref[...]
        v2 = v * v
        t = jnp.tanh(c0 * (v + 0.044715 * (v2 * v)))
        half = 0.5 * (1.0 + t)
        hid_ref[rows] = (v * half).astype(BF16)
        slope = half + 0.5 * v * (1.0 - t * t) * (c0 * (1.0 + 0.134145 * v2))
        grad = cot_ref[rows].astype(F32) * slope
        grad_bf = grad.astype(BF16)
        rt[rep, :, rows] = mm_nt(weight, grad_bf).astype(BF16)
        wsum = wsum + mm_tn(agg, grad_bf)
        bsum = bsum + jnp.sum(grad.reshape(32, 8, 256), axis=0)
        return wsum, bsum

    carry = (jnp.zeros((128, 256), F32), jnp.zeros((8, 256), F32))
    for h in range(2):
        carry = epilogue(h, carry)
    wsum, bsum = carry

    def put(i, src, dst):
        copy = pltpu.make_async_copy(src, dst, out_sem.at[i])
        copy.start()
        sent.append(copy.wait)

    def rows_copy(k):
        return send(rt.at[rep], rt.at[rep], rt_s.at[k], rt_r.at[k], rep_peer(k))

    def pass_on():
        far = rt.at[lax.rem(yh + 1, 2) * 2 + core]
        return send(far, far, rt_s.at[3], rt_r.at[3], rep_peer(1))

    for k in (2, 1):
        rows_copy(k).start()
        sent.append(rows_copy(k).wait_send)

    put(0, hid_ref, hid_hbm)

    for j in range(16):
        wa_s[j] = wsum[j * 8 : j * 8 + 8]
    ba_s[...] = bsum
    first = a_pos == 0

    def wa_copy(k):
        return send(wa_s.at[a_at(k)], wa.at[a_pos], wa_ss.at[k], wa_rs.at[k], a_peer(k))

    def ba_copy():
        return send(ba_s, ba.at[a_pos], ba_ss, ba_rs.at[a_pos], device(0, 0, z, 0, core))

    for k in range(1, 16):
        wa_copy(k).start()
        sent.append(wa_copy(k).wait_send)
    wa[a_pos] = wa_s[a_pos]

    @pl.when(a_pos > 0)
    def _():
        ba_copy().start()

    @pl.when(first)
    def _():
        ba[0] = bsum

    def ba_drain():
        @pl.when(a_pos > 0)
        def _():
            ba_copy().wait_send()

    sent.append(ba_drain)

    def wb_copy(k):
        return send(wb.at[b_pos], wb.at[b_pos], wb_ss.at[k], wb_rs.at[k], b_peer(k))

    def bb_copy(k):
        return send(bb.at[b_pos], bb.at[b_pos], bb_ss.at[k], bb_rs.at[k], b_peer(k))

    def add_up(ref):
        total = ref[0]
        for j in range(1, 16):
            total = total + ref[j]
        return total

    def step_b():
        for k in range(1, 16):
            arrived(wa.at[lax.rem(a_pos - k + 16, 16)], wa_rs.at[k])
        wb[b_pos] = add_up(wa)
        for k in range(1, 16):
            wb_copy(k).start()
            sent.append(wb_copy(k).wait_send)

        @pl.when(first)
        def _():
            for j in range(1, 16):
                arrived(ba.at[j], ba_rs.at[j])
            bb[b_pos] = add_up(ba)
            for k in range(1, 16):
                bb_copy(k).start()

        sent.append(functools.partial(drain_first, bb_copy))

    def drain_first(copy):
        @pl.when(first)
        def _():
            for k in range(1, 16):
                copy(k).wait_send()

    def wc_copy(k):
        return send(wc.at[a_pos], wc.at[a_pos], wc_ss.at[k], wc_rs.at[k], a_peer(k))

    def bc_copy(k):
        return send(bc, bc, bc_ss.at[k], bc_rs, a_peer(k))

    def step_c():
        for k in range(1, 16):
            arrived(wb.at[lax.rem(b_pos - k + 16, 16)], wb_rs.at[k])
        wc[a_pos] = add_up(wb) * scale
        for k in range(1, 16):
            wc_copy(k).start()
            sent.append(wc_copy(k).wait_send)

        @pl.when(first)
        def _():
            for k in range(1, 16):
                arrived(bb.at[lax.rem(b_pos - k + 16, 16)], bb_rs.at[k])
            total = jnp.sum(add_up(bb), axis=0, keepdims=True) * scale
            bc[...] = jnp.broadcast_to(total, (8, 256))
            for k in range(1, 16):
                bc_copy(k).start()

        sent.append(functools.partial(drain_first, bc_copy))

    def quarter_of(k):
        return lax.rem(yh + k // 2, 2) * 2 + lax.rem(core + k % 2, 2)

    def back_terms(s, q, quarter):
        left = rt[quarter]
        out = mm(left[:, :256], adj[tab[s * 64 + quarter * 16 + q]])
        return out + mm(left[:, 256:], adj[tab[s * 64 + quarter * 16 + 8 + q]])

    def back_own(i, carry):
        s, q = lax.div(i, 8), lax.rem(i, 8)
        acct[s, q] = back_terms(s, q, quarter_of(0))
        return carry

    lax.fori_loop(0, 16, back_own, 0, unroll=4)
    arrived(rt.at[quarter_of(1)], rt_r.at[1])

    def back_core(i, carry):
        s, q = lax.div(i, 8), lax.rem(i, 8)
        acct[s, q] += back_terms(s, q, quarter_of(1))
        return carry

    lax.fori_loop(0, 16, back_core, 0, unroll=4)
    arrived(rt.at[quarter_of(2)], rt_r.at[2])
    pass_on().start()
    sent.append(pass_on().wait_send)

    def back_far(i, carry):
        s, q = lax.div(i, 8), lax.rem(i, 8)
        acct[s, q] += back_terms(s, q, quarter_of(2))
        return carry

    lax.fori_loop(0, 16, back_far, 0, unroll=4)
    step_b()
    arrived(rt.at[quarter_of(3)], rt_r.at[3])

    def xs_copy(s, k):
        px, pyl = xy_at(k)
        return send(xs.at[s, pyl * 4 + px], xr.at[s, k], xs_s.at[s, k], xs_r.at[s, k], xy_peer(k))

    for s in range(2):
        for hk in (1, 0):
            half = lax.rem(yl + hk, 2)

            def back_rest(zz, carry):
                q = half * 4 + zz
                total = acct[s, q] + back_terms(s, q, quarter_of(3))
                out = total.T.astype(BF16)
                for zl in range(2):
                    for px in range(4):
                        at = zl * 128 + px * 32
                        xs[s, half * 4 + px, zz * 2 + zl] = out[at : at + 32]
                return carry

            lax.fori_loop(0, 4, back_rest, 0, unroll=True)
            for k in (1, 3, 2) if hk == 0 else (4, 5, 7, 6):
                xs_copy(s, k).start()
                sent.append(xs_copy(s, k).wait_send)

    step_c()

    def zs_copy(s, k):
        return send(zs.at[s, lax.rem(z + k, 8)], zr.at[s, k], zs_s.at[s, k], zs_r.at[s, k], z_peer(k))

    for s in range(2):
        for k in range(1, 8):
            arrived(xr.at[s, k], xs_r.at[s, k])
        for zz in range(8):
            total = xs[s, my_j, zz].astype(F32)
            for k in range(1, 8):
                total += xr[s, k, zz].astype(F32)
            zs[s, zz] = total.astype(BF16)
        for k in (4, 3, 5, 2, 6, 1, 7):
            zs_copy(s, k).start()
            sent.append(zs_copy(s, k).wait_send)

    for s in range(2):
        total = zs[s, z].astype(F32)
        for k in range(1, 8):
            arrived(zr.at[s, k], zs_r.at[s, k])
            total += zr[s, k].astype(F32)
        gin_ref[s] = total.astype(BF16)
    put(1, gin_ref, gin_hbm)

    for k in range(1, 16):
        arrived(wc.at[lax.rem(a_pos - k + 16, 16)], wc_rs.at[k])
    put(2, wc, gw_hbm)

    @pl.when(a_pos > 0)
    def _():
        arrived(bc, bc_rs)

    gb_ref[...] = bc[pl.ds(0, 1)]
    put(3, gb_ref, gb_hbm)

    for drain in sent:
        drain()


def layer(features, adjacency, table, weight, bias, cotangent, scale):
    hbm = pl.BlockSpec(memory_space=pltpu.HBM)
    sems = [
        (4,), (3,), (4,), (2, 8), (2, 8), (2, 8), (2,), (2, 8), (4,), (4,), (4,), (4,),
        (16,), (16,), (16,), (16,), (16,), (16,), (), (16,), (16,), (16,), (16,), (),
        (2, 8), (2, 8), (2, 8), (2, 8),
    ]
    return pl.pallas_call(
        functools.partial(kernel, scale),
        name="layer",
        out_shape=(
            jax.ShapeDtypeStruct((512, 256), BF16),
            jax.ShapeDtypeStruct((2, 32, 128), BF16),
            jax.ShapeDtypeStruct((16, 8, 256), F32),
            jax.ShapeDtypeStruct((1, 256), F32),
        ),
        in_specs=[hbm, hbm, pl.BlockSpec(memory_space=pltpu.SMEM), hbm, hbm, hbm],
        out_specs=(hbm, hbm, hbm, hbm),
        scratch_shapes=[
            pltpu.VMEM((SLOTS + 1, 256, 256), BF16),
            pltpu.VMEM((2, 8, 256, 128), BF16),
            pltpu.VMEM((8, 256, 128), F32),
            pltpu.VMEM((2, 2, 256, 128), F32),
            pltpu.VMEM((2, 256, 128), BF16),
            pltpu.VMEM((2, 256, 128), BF16),
            pltpu.VMEM((4, 128, 512), BF16),
            pltpu.VMEM((2, 8, 128, 256), F32),
            pltpu.VMEM((2, 8, 8, 32, 128), BF16),
            pltpu.VMEM((2, 8, 8, 32, 128), BF16),
            pltpu.VMEM((2, 8, 32, 128), BF16),
            pltpu.VMEM((2, 8, 32, 128), BF16),
            pltpu.VMEM((128, 256), BF16),
            pltpu.VMEM((1, 256), F32),
            pltpu.VMEM((512, 256), BF16),
            pltpu.VMEM((512, 256), BF16),
            pltpu.VMEM((2, 32, 128), BF16),
            pltpu.VMEM((1, 256), F32),
            pltpu.VMEM((16, 8, 256), F32),
            pltpu.VMEM((16, 8, 256), F32),
            pltpu.VMEM((16, 8, 256), F32),
            pltpu.VMEM((16, 8, 256), F32),
            pltpu.VMEM((8, 256), F32),
            pltpu.VMEM((16, 8, 256), F32),
            pltpu.VMEM((16, 8, 256), F32),
            pltpu.VMEM((8, 256), F32),
        ]
        + [pltpu.SemaphoreType.DMA(shape) for shape in sems],
        compiler_params=pltpu.CompilerParams(
            collective_id=1, has_side_effects=True, vmem_limit_bytes=VMEM_BYTES
        ),
    )(features, adjacency, table, weight, bias, cotangent)


def finish_kernel(n, *refs):
    ins, outs, held, sem = refs[:n], refs[n : 2 * n], refs[2 * n : 3 * n], refs[3 * n]
    loads = [pltpu.make_async_copy(ins[i], held[i], sem.at[0, i]) for i in range(n)]
    stores = [pltpu.make_async_copy(held[i], outs[i], sem.at[1, i]) for i in range(n)]
    for copy in loads:
        copy.start()
    for load, store in zip(loads, stores):
        load.wait()
        store.start()
    for copy in stores:
        copy.wait()


def finish(*arrays):
    n = len(arrays)
    hbm = pl.BlockSpec(memory_space=pltpu.HBM)
    return pl.pallas_call(
        functools.partial(finish_kernel, n),
        name="finish",
        out_shape=tuple(jax.ShapeDtypeStruct(a.shape, a.dtype) for a in arrays),
        in_specs=[hbm] * n,
        out_specs=(hbm,) * n,
        scratch_shapes=[pltpu.VMEM(a.shape, a.dtype) for a in arrays]
        + [pltpu.SemaphoreType.DMA((2, n))],
        compiler_params=pltpu.CompilerParams(vmem_limit_bytes=VMEM_BYTES),
    )(*arrays)


def shards(features, adjacency, tile_coords, tile_counts, weight, bias, cotangent):
    rows_count = lax.axis_size("rows")
    scale = 1.0 / math.sqrt(features.shape[0] * rows_count)
    coords = tile_coords[0, 0]
    counts = tile_counts[0, 0]
    slot = jnp.arange(40, dtype=jnp.int32)
    place = jnp.where(slot[None, :] < counts[:, None], coords[:, 0] * 8 + coords[:, 1], -1)
    hit = place[:, None, :] == jnp.arange(64, dtype=jnp.int32)[None, :, None]
    number = slot[None, None, :] + 40 * jnp.arange(2, dtype=jnp.int32)[:, None, None] - SLOTS
    table = SLOTS + jnp.sum(jnp.where(hit, number, 0), axis=2)
    hidden, grad_inputs, grad_weight, grad_bias = layer(
        features,
        adjacency.reshape(SLOTS, 256, 256),
        table.reshape(128),
        weight,
        bias.reshape(1, 256),
        cotangent,
        scale,
    )
    hidden, grad_inputs, grad_weight, grad_bias = finish(
        hidden, grad_inputs, grad_weight, grad_bias
    )
    return hidden, grad_inputs[None], grad_weight.reshape(128, 256), grad_bias.reshape(256)


def solution(mesh):
    return jax.shard_map(
        shards,
        mesh=mesh,
        in_specs=(
            P("rows", None),
            P("rows", "rep", None, None, None, None),
            P("rows", "rep", None, None, None),
            P("rows", "rep", None),
            P(),
            P(),
            P(("rows", "rep"), None),
        ),
        out_specs=(P(("rows", "rep"), None), P("rep", None, "rows", None), P(), P()),
        check_vma=False,
    )
```

```python
import functools
import math

import jax
import jax.numpy as jnp
from jax import lax
from jax.experimental import pallas as pl
from jax.experimental.pallas import tpu as pltpu
from jax.sharding import PartitionSpec as P

MESH = pl.DeviceIdType.MESH
F32 = jnp.float32
BF16 = jnp.bfloat16
SLOTS = 80
CHUNKS = (4, 1)
KEEP = (32, 16)
VMEM_BYTES = 62 * 2**20
XY_ORDER = (1, 3, 4, 5, 7, 2, 6)


def mm(a, b):
    return lax.dot_general(a, b, (((1,), (0,)), ((), ())), preferred_element_type=F32)


def mm_nt(a, b):
    return lax.dot_general(a, b, (((1,), (1,)), ((), ())), preferred_element_type=F32)


def mm_tn(a, b):
    return lax.dot_general(a, b, (((0,), (0,)), ((), ())), preferred_element_type=F32)


def arrived(ref, sem):
    pltpu.make_async_copy(ref, ref, sem).wait()


def kernel(
    scale,
    feat_hbm, adj_hbm, coord_hbm, count_hbm, w_hbm, b_hbm, cot_hbm,
    hid_hbm, gin_hbm, gw_hbm, gb_hbm,
    coord, count, place, line, tab, adj, feat, acc, pf, ps, pr, rt, acct, xs0, xs1, xr0, xr1, xa, zs, zr, zf, yf, yr,
    w_ref, b_ref, cot_ref, hid_ref, gin_ref, gb_ref, wa_s, wa, wb, wc, ba_s, ba, bb, bc,
    adj_sem, in_sem, tab_sem, out_sem, s1, s2, s3, r12, r3, ps_s, ps_r, rt_s, rt_r,
    wa_ss, wa_rs, wb_ss, wb_rs, wc_ss, wc_rs,
    ba_ss, ba_rs, bb_ss, bb_rs, bc_ss, bc_rs, xs_s, xs_r, zs_s, zs_r,
    zf_s, zf_r, yf_s, yf_r,
):
    row = lax.axis_index("rows")
    rep = lax.axis_index("rep")
    x = lax.rem(row, 4)
    z = lax.rem(lax.div(row, 4), 8)
    yl = lax.div(row, 32)
    yh = lax.div(rep, 2)
    core = lax.rem(rep, 2)

    def device(x, yl, z, yh, core):
        return (yl * 32 + z * 4 + x, yh * 2 + core)

    def xy_at(k, sign=1):
        return lax.rem(x + sign * (k % 4) + 4, 4), lax.rem(yl + k // 4, 2)

    def xy_peer(k):
        px, pyl = xy_at(k)
        return device(px, pyl, z, yh, core)

    def z_peer(k):
        return device(x, yl, lax.rem(z + k, 8), yh, core)

    def rep_peer(k):
        return device(x, yl, z, lax.rem(yh + k // 2, 2), lax.rem(core + k % 2, 2))

    a_pos = (yh * 2 + yl) * 4 + x
    b_pos = z * 2 + core

    def a_at(k):
        return lax.rem(a_pos + k, 16)

    def a_peer(k):
        pos = a_at(k)
        py = lax.div(pos, 4)
        return device(lax.rem(pos, 4), lax.rem(py, 2), z, lax.div(py, 2), core)

    def b_peer(k):
        pos = lax.rem(b_pos + k, 16)
        return device(x, yl, lax.div(pos, 2), yh, lax.rem(pos, 2))

    def send(src, dst, send_sem, recv_sem, peer):
        return pltpu.make_async_remote_copy(
            src_ref=src, dst_ref=dst, send_sem=send_sem, recv_sem=recv_sem,
            device_id=peer, device_id_type=MESH,
        )

    sent = []

    barrier = pltpu.get_barrier_semaphore()
    greet = [a_peer(k) for k in range(1, 16)]
    greet += [b_peer(k) for k in range(1, 16)]
    for peer in greet:
        pl.semaphore_signal(barrier, inc=1, device_id=peer, device_id_type=MESH)
    part = SLOTS // 4
    for i in range(4):
        pltpu.make_async_copy(
            adj_hbm.at[pl.ds(i * part, part)], adj.at[pl.ds(i * part, part)], adj_sem.at[i]
        ).start()

    small = [(coord_hbm, coord), (count_hbm, count), (w_hbm, w_ref), (b_hbm, b_ref), (cot_hbm, cot_ref)]
    for i, (src, dst) in enumerate(small):
        pltpu.make_async_copy(src, dst, in_sem.at[i]).start()

    pl.semaphore_wait(barrier, len(greet))

    my_j = yl * 4 + x
    is_root = [row == (rep * 2 + s) * 8 for s in range(2)]
    in_plane = [z == core * 4 + s * 2 for s in range(2)]

    def span(s, c):
        size = 256 // CHUNKS[s]
        return pl.ds(c * size, size)

    def root_copy(s, c, k):
        px, pyl = xy_at(k)
        j = pyl * 4 + px
        size = 256 // CHUNKS[s]
        return send(
            feat_hbm.at[pl.ds(pl.multiple_of(j * 256 + c * size, size), size)], feat.at[s, j, span(s, c)],
            s1.at[s, c, k], r12.at[s, c], device(px, pyl, z, yh, core),
        )

    def plane_copy(s, c, k):
        mine = feat.at[s, my_j, span(s, c)]
        return send(mine, mine, s2.at[s, c, k], r12.at[s, c], z_peer(k))

    def side_copy(s, c, k):
        mine = feat.at[s, my_j, span(s, c)]
        return send(mine, mine, s3.at[s, c, k], r3.at[s, c, k], xy_peer(k))

    def drain_if(cond, copy, s):
        @pl.when(cond)
        def _():
            for c in range(CHUNKS[s]):
                for k in range(1, 8):
                    copy(s, c, k).wait_send()

    for s in range(2):
        @pl.when(is_root[s])
        def _():
            for c in range(CHUNKS[s]):
                size = 256 // CHUNKS[s]
                for k in XY_ORDER:
                    root_copy(s, c, k).start()
                pltpu.make_async_copy(
                    feat_hbm.at[pl.ds(pl.multiple_of(my_j * 256 + c * size, size), size)],
                    feat.at[s, my_j, span(s, c)], r12.at[s, c],
                ).start()

        sent.append(functools.partial(drain_if, is_root[s], root_copy, s))

    acc[...] = jnp.zeros_like(acc)
    adj[SLOTS] = jnp.zeros((256, 256), BF16)

    for i, (src, dst) in enumerate(small):
        arrived(dst, in_sem.at[i])
    place[...] = jnp.full((8, 128), -1, jnp.int32)
    slot = lax.broadcasted_iota(jnp.int32, (1, 40), 1)
    for s in range(2):
        where = coord[s, pl.ds(0, 1)] * 8 + coord[s, pl.ds(1, 1)] + s * 64
        place[pl.ds(s, 1), pl.ds(0, 40)] = jnp.where(slot < count[:, s : s + 1], where, -1)
    by_slot = place[...].T
    spot = lax.broadcasted_iota(jnp.int32, (128, 128), 1)
    number = lax.broadcasted_iota(jnp.int32, (128, 128), 0) - SLOTS
    found = jnp.where(by_slot[:, 0:1] == spot, number, 0)
    found += jnp.where(by_slot[:, 1:2] == spot, number + 40, 0)
    line[...] = jnp.sum(found, axis=0, keepdims=True) + SLOTS
    to_scalar = pltpu.make_async_copy(line, tab, tab_sem)
    to_scalar.start()
    to_scalar.wait()

    for s in range(2):
        @pl.when(in_plane[s])
        def _():
            for c in range(CHUNKS[s]):
                arrived(feat.at[s, my_j, span(s, c)], r12.at[s, c])
                for k in (4, 3, 5, 2, 6, 1, 7):
                    plane_copy(s, c, k).start()

        sent.append(functools.partial(drain_if, in_plane[s], plane_copy, s))

    for s in range(2):
        for c in range(CHUNKS[s]):
            @pl.when(jnp.logical_not(in_plane[s]))
            def _():
                arrived(feat.at[s, my_j, span(s, c)], r12.at[s, c])

            for k in XY_ORDER:
                side_copy(s, c, k).start()
                sent.append(side_copy(s, c, k).wait_send)

    for i in range(4):
        view = adj.at[pl.ds(i * part, part)]
        arrived(view, adj_sem.at[i])

    def forward(s, k, carry):
        fx = lax.rem(x - lax.rem(k, 4) + 4, 4)
        fyl = lax.rem(yl + lax.div(k, 4), 2)
        j = fyl * 4 + fx

        @pl.when(k > 0)
        def _():
            for c in range(CHUNKS[s]):
                arrived(feat.at[s, j, span(s, c)], r3.at[s, c, k])

        column = feat[s, j]
        for p in range(8):
            acc[p] += mm(adj[tab[0, s * 64 + p * 8 + j]], column)
        return carry

    for s in range(2):
        lax.fori_loop(0, 8, functools.partial(forward, s), 0)

    far_yh, other = lax.rem(yh + 1, 2), lax.rem(core + 1, 2)

    def core_copy(i):
        quarter = (far_yh, yh)[i] * 2 + other
        return send(acc.at[pl.ds(quarter * 2, 2)], pf.at[i], ps_s.at[i], ps_r.at[i], rep_peer(1))

    def far_copy(h):
        return send(ps.at[h], pr.at[h], ps_s.at[2 + h], ps_r.at[2 + h], rep_peer(2))

    for i in range(2):
        core_copy(i).start()
        sent.append(core_copy(i).wait_send)
    arrived(pf.at[0], ps_r.at[0])
    for h in range(2):
        ps[h] = (acc[(far_yh * 2 + core) * 2 + h] + pf[0, h]).astype(BF16)
        far_copy(h).start()
        sent.append(far_copy(h).wait_send)
    arrived(pf.at[1], ps_r.at[1])

    c0 = math.sqrt(2.0 / math.pi)
    weight = w_ref[...]

    def epilogue(h, carry):
        wsum, bsum = carry
        rows = pl.ds(pl.multiple_of(h * 256, 256), 256)
        total = acc[rep * 2 + h] + pf[1, h]
        arrived(pr.at[h], ps_r.at[2 + h])
        total += pr[h].astype(F32)
        agg = total.astype(BF16)
        v = mm(agg, weight) + b_ref[...]
        v2 = v * v
        t = jnp.tanh(c0 * (v + 0.044715 * (v2 * v)))
        half = 0.5 * (1.0 + t)
        hid_ref[rows] = (v * half).astype(BF16)
        slope = half + 0.5 * v * (1.0 - t * t) * (c0 * (1.0 + 0.134145 * v2))
        grad = cot_ref[rows].astype(F32) * slope
        grad_bf = grad.astype(BF16)
        rt[rep, :, rows] = mm_nt(weight, grad_bf).astype(BF16)
        wsum = wsum + mm_tn(agg, grad_bf)
        bsum = bsum + jnp.sum(grad.reshape(32, 8, 256), axis=0)
        return wsum, bsum

    carry = (jnp.zeros((128, 256), F32), jnp.zeros((8, 256), F32))
    for h in range(2):
        carry = epilogue(h, carry)
    wsum, bsum = carry

    def put(i, src, dst):
        copy = pltpu.make_async_copy(src, dst, out_sem.at[i])
        copy.start()
        sent.append(copy.wait)

    def rows_copy(k):
        return send(rt.at[rep], rt.at[rep], rt_s.at[k], rt_r.at[k], rep_peer(k))

    def pass_on():
        far = rt.at[lax.rem(yh + 1, 2) * 2 + core]
        return send(far, far, rt_s.at[3], rt_r.at[3], rep_peer(1))

    for k in (2, 1):
        rows_copy(k).start()
        sent.append(rows_copy(k).wait_send)

    put(0, hid_ref, hid_hbm)

    for j in range(16):
        wa_s[j] = wsum[j * 8 : j * 8 + 8]
    ba_s[...] = bsum
    first = a_pos == 0

    def wa_copy(k):
        return send(wa_s.at[a_at(k)], wa.at[a_pos], wa_ss.at[k], wa_rs.at[k], a_peer(k))

    def ba_copy():
        return send(ba_s, ba.at[a_pos], ba_ss, ba_rs.at[a_pos], device(0, 0, z, 0, core))

    for k in range(1, 16):
        wa_copy(k).start()
        sent.append(wa_copy(k).wait_send)
    wa[a_pos] = wa_s[a_pos]

    @pl.when(a_pos > 0)
    def _():
        ba_copy().start()

    @pl.when(first)
    def _():
        ba[0] = bsum

    def ba_drain():
        @pl.when(a_pos > 0)
        def _():
            ba_copy().wait_send()

    sent.append(ba_drain)

    def wb_copy(k):
        return send(wb.at[b_pos], wb.at[b_pos], wb_ss.at[k], wb_rs.at[k], b_peer(k))

    def bb_copy(k):
        return send(bb.at[b_pos], bb.at[b_pos], bb_ss.at[k], bb_rs.at[k], b_peer(k))

    def add_up(ref):
        total = ref[0]
        for j in range(1, 16):
            total = total + ref[j]
        return total

    def step_b():
        for k in range(1, 16):
            arrived(wa.at[lax.rem(a_pos - k + 16, 16)], wa_rs.at[k])
        wb[b_pos] = add_up(wa)
        for k in range(1, 16):
            wb_copy(k).start()
            sent.append(wb_copy(k).wait_send)

        @pl.when(first)
        def _():
            for j in range(1, 16):
                arrived(ba.at[j], ba_rs.at[j])
            bb[b_pos] = add_up(ba)
            for k in range(1, 16):
                bb_copy(k).start()

        sent.append(functools.partial(drain_first, bb_copy))

    def drain_first(copy):
        @pl.when(first)
        def _():
            for k in range(1, 16):
                copy(k).wait_send()

    def wc_copy(k):
        return send(wc.at[a_pos], wc.at[a_pos], wc_ss.at[k], wc_rs.at[k], a_peer(k))

    def bc_copy(k):
        return send(bc, bc, bc_ss.at[k], bc_rs, a_peer(k))

    def step_c():
        for k in range(1, 16):
            arrived(wb.at[lax.rem(b_pos - k + 16, 16)], wb_rs.at[k])
        wc[a_pos] = add_up(wb) * scale
        for k in range(1, 16):
            wc_copy(k).start()
            sent.append(wc_copy(k).wait_send)

        @pl.when(first)
        def _():
            for k in range(1, 16):
                arrived(bb.at[lax.rem(b_pos - k + 16, 16)], bb_rs.at[k])
            total = jnp.sum(add_up(bb), axis=0, keepdims=True) * scale
            bc[...] = jnp.broadcast_to(total, (8, 256))
            for k in range(1, 16):
                bc_copy(k).start()

        sent.append(functools.partial(drain_first, bc_copy))

    def quarter_of(k):
        return lax.rem(yh + k // 2, 2) * 2 + lax.rem(core + k % 2, 2)

    def back_terms(s, q, quarter):
        left = rt[quarter]
        out = mm(left[:, :256], adj[tab[0, s * 64 + quarter * 16 + q]])
        return out + mm(left[:, 256:], adj[tab[0, s * 64 + quarter * 16 + 8 + q]])

    def back_own(i, carry):
        s, q = lax.div(i, 8), lax.rem(i, 8)
        acct[s, q] = back_terms(s, q, quarter_of(0))
        return carry

    lax.fori_loop(0, 16, back_own, 0, unroll=4)
    arrived(rt.at[quarter_of(1)], rt_r.at[1])

    def back_core(i, carry):
        s, q = lax.div(i, 8), lax.rem(i, 8)
        acct[s, q] += back_terms(s, q, quarter_of(1))
        return carry

    lax.fori_loop(0, 16, back_core, 0, unroll=4)
    arrived(rt.at[quarter_of(2)], rt_r.at[2])
    pass_on().start()
    sent.append(pass_on().wait_send)

    def back_far(i, carry):
        s, q = lax.div(i, 8), lax.rem(i, 8)
        acct[s, q] += back_terms(s, q, quarter_of(2))
        return carry

    step_b()
    lax.fori_loop(0, 16, back_far, 0, unroll=4)
    arrived(rt.at[quarter_of(3)], rt_r.at[3])

    xs, xr = (xs0, xs1), (xr0, xr1)

    def xs_copy(s, k):
        px, pyl = xy_at(k)
        return send(xs[s].at[pyl * 4 + px], xr[s].at[k], xs_s.at[s, k], xs_r.at[s, k], xy_peer(k))

    late = pl.ds(KEEP[1], 32 - KEEP[1])

    def zf_copy(k):
        return send(xa.at[lax.rem(z + k, 8)], zf.at[k], zf_s.at[k], zf_r.at[k], z_peer(k))

    def yf_copy(k):
        px, pyl = xy_at(k)
        return send(yf.at[pyl * 4 + px], yr.at[k], yf_s.at[k], yf_r.at[k], xy_peer(k))

    for s in range(2):
        for hk in (1, 0):
            half = lax.rem(yl + hk, 2)

            def back_rest(zz, carry):
                q = half * 4 + zz
                total = acct[s, q] + back_terms(s, q, quarter_of(3))
                out = total.T.astype(BF16)
                for zl in range(2):
                    for px in range(4):
                        at = zl * 128 + px * 32
                        keep = KEEP[s]
                        xs[s][half * 4 + px, zz * 2 + zl] = out[at : at + keep]
                        if s == 1:
                            xa[zz * 2 + zl, half * 4 + px] = out[at + keep : at + 32]
                return carry

            lax.fori_loop(0, 4, back_rest, 0, unroll=True)
            for k in (1, 3, 2) if hk == 0 else (4, 5, 7, 6):
                xs_copy(s, k).start()
                sent.append(xs_copy(s, k).wait_send)
    for k in (4, 3, 5, 2, 6, 1, 7):
        zf_copy(k).start()
        sent.append(zf_copy(k).wait_send)

    step_c()

    def zs_copy(s, k):
        rows = pl.ds(0, KEEP[s])
        return send(
            zs.at[s, lax.rem(z + k, 8), rows], zr.at[s, k, rows], zs_s.at[s, k], zs_r.at[s, k], z_peer(k)
        )

    def over_xy(s):
        rows = pl.ds(0, KEEP[s])
        for k in range(1, 8):
            arrived(xr[s].at[k], xs_r.at[s, k])
        for zz in range(8):
            total = xs[s][my_j, zz].astype(F32)
            for k in range(1, 8):
                total += xr[s][k, zz].astype(F32)
            zs[s, zz, rows] = total.astype(BF16)
        for k in (4, 3, 5, 2, 6, 1, 7):
            zs_copy(s, k).start()
            sent.append(zs_copy(s, k).wait_send)

    over_xy(0)
    for k in range(1, 8):
        arrived(zf.at[k], zf_r.at[k])
    for j in range(8):
        total = xa[z, j].astype(F32)
        for k in range(1, 8):
            total += zf[k, j].astype(F32)
        yf[j] = total.astype(BF16)
    for k in XY_ORDER:
        yf_copy(k).start()
        sent.append(yf_copy(k).wait_send)
    over_xy(1)

    for s in range(2):
        rows = pl.ds(0, KEEP[s])
        total = zs[s, z, rows].astype(F32)
        for k in range(1, 8):
            arrived(zr.at[s, k, rows], zs_r.at[s, k])
            total += zr[s, k, rows].astype(F32)
        gin_ref[s, rows] = total.astype(BF16)
    total = yf[my_j].astype(F32)
    for k in range(1, 8):
        arrived(yr.at[k], yf_r.at[k])
        total += yr[k].astype(F32)
    gin_ref[1, late] = total.astype(BF16)
    put(1, gin_ref, gin_hbm)

    for k in range(1, 16):
        arrived(wc.at[lax.rem(a_pos - k + 16, 16)], wc_rs.at[k])
    put(2, wc, gw_hbm)

    @pl.when(a_pos > 0)
    def _():
        arrived(bc, bc_rs)

    gb_ref[...] = bc[pl.ds(0, 1)]
    put(3, gb_ref, gb_hbm)

    for drain in sent:
        drain()


def layer(features, adjacency, coords, counts, weight, bias, cotangent, scale):
    hbm = pl.BlockSpec(memory_space=pltpu.HBM)
    sems = [
        (4,), (5,), (), (4,), (2, 4, 8), (2, 4, 8), (2, 4, 8), (2, 4), (2, 4, 8), (4,), (4,), (4,), (4,),
        (16,), (16,), (16,), (16,), (16,), (16,), (), (16,), (16,), (16,), (16,), (),
        (2, 8), (2, 8), (2, 8), (2, 8), (8,), (8,), (8,), (8,),
    ]
    return pl.pallas_call(
        functools.partial(kernel, scale),
        name="layer",
        out_shape=(
            jax.ShapeDtypeStruct((512, 256), BF16),
            jax.ShapeDtypeStruct((2, 32, 128), BF16),
            jax.ShapeDtypeStruct((16, 8, 256), F32),
            jax.ShapeDtypeStruct((1, 256), F32),
        ),
        in_specs=[hbm] * 7,
        out_specs=(hbm, hbm, hbm, hbm),
        scratch_shapes=[
            pltpu.VMEM((2, 2, 40), jnp.int32),
            pltpu.VMEM((1, 2), jnp.int32),
            pltpu.VMEM((8, 128), jnp.int32),
            pltpu.VMEM((1, 128), jnp.int32),
            pltpu.SMEM((1, 128), jnp.int32),
            pltpu.VMEM((SLOTS + 1, 256, 256), BF16),
            pltpu.VMEM((2, 8, 256, 128), BF16),
            pltpu.VMEM((8, 256, 128), F32),
            pltpu.VMEM((2, 2, 256, 128), F32),
            pltpu.VMEM((2, 256, 128), BF16),
            pltpu.VMEM((2, 256, 128), BF16),
            pltpu.VMEM((4, 128, 512), BF16),
            pltpu.VMEM((2, 8, 128, 256), F32),
            pltpu.VMEM((8, 8, KEEP[0], 128), BF16),
            pltpu.VMEM((8, 8, KEEP[1], 128), BF16),
            pltpu.VMEM((8, 8, KEEP[0], 128), BF16),
            pltpu.VMEM((8, 8, KEEP[1], 128), BF16),
            pltpu.VMEM((8, 8, 32 - KEEP[1], 128), BF16),
            pltpu.VMEM((2, 8, 32, 128), BF16),
            pltpu.VMEM((2, 8, 32, 128), BF16),
            pltpu.VMEM((8, 8, 16, 128), BF16),
            pltpu.VMEM((8, 16, 128), BF16),
            pltpu.VMEM((8, 16, 128), BF16),
            pltpu.VMEM((128, 256), BF16),
            pltpu.VMEM((1, 256), F32),
            pltpu.VMEM((512, 256), BF16),
            pltpu.VMEM((512, 256), BF16),
            pltpu.VMEM((2, 32, 128), BF16),
            pltpu.VMEM((1, 256), F32),
            pltpu.VMEM((16, 8, 256), F32),
            pltpu.VMEM((16, 8, 256), F32),
            pltpu.VMEM((16, 8, 256), F32),
            pltpu.VMEM((16, 8, 256), F32),
            pltpu.VMEM((8, 256), F32),
            pltpu.VMEM((16, 8, 256), F32),
            pltpu.VMEM((16, 8, 256), F32),
            pltpu.VMEM((8, 256), F32),
        ]
        + [pltpu.SemaphoreType.DMA(shape) for shape in sems],
        compiler_params=pltpu.CompilerParams(
            collective_id=1, has_side_effects=True, vmem_limit_bytes=VMEM_BYTES
        ),
    )(features, adjacency, coords, counts, weight, bias, cotangent)


def finish_kernel(n, *refs):
    ins, outs, held, sem = refs[:n], refs[n : 2 * n], refs[2 * n : 3 * n], refs[3 * n]
    loads = [pltpu.make_async_copy(ins[i], held[i], sem.at[0, i]) for i in range(n)]
    stores = [pltpu.make_async_copy(held[i], outs[i], sem.at[1, i]) for i in range(n)]
    for copy in loads:
        copy.start()
    for load, store in zip(loads, stores):
        load.wait()
        store.start()
    for copy in stores:
        copy.wait()


def finish(*arrays):
    n = len(arrays)
    hbm = pl.BlockSpec(memory_space=pltpu.HBM)
    return pl.pallas_call(
        functools.partial(finish_kernel, n),
        name="finish",
        out_shape=tuple(jax.ShapeDtypeStruct(a.shape, a.dtype) for a in arrays),
        in_specs=[hbm] * n,
        out_specs=(hbm,) * n,
        scratch_shapes=[pltpu.VMEM(a.shape, a.dtype) for a in arrays]
        + [pltpu.SemaphoreType.DMA((2, n))],
        compiler_params=pltpu.CompilerParams(vmem_limit_bytes=VMEM_BYTES),
    )(*arrays)


def shards(features, adjacency, tile_coords, tile_counts, weight, bias, cotangent):
    rows_count = lax.axis_size("rows")
    scale = 1.0 / math.sqrt(features.shape[0] * rows_count)
    hidden, grad_inputs, grad_weight, grad_bias = layer(
        features,
        adjacency.reshape(SLOTS, 256, 256),
        tile_coords.reshape(2, 2, 40),
        tile_counts.reshape(1, 2),
        weight,
        bias.reshape(1, 256),
        cotangent,
        scale,
    )
    hidden, grad_inputs, grad_weight, grad_bias = finish(
        hidden, grad_inputs, grad_weight, grad_bias
    )
    return hidden, grad_inputs[None], grad_weight.reshape(128, 256), grad_bias.reshape(256)


def solution(mesh):
    return jax.shard_map(
        shards,
        mesh=mesh,
        in_specs=(
            P("rows", None),
            P("rows", "rep", None, None, None, None),
            P("rows", "rep", None, None, None),
            P("rows", "rep", None),
            P(),
            P(),
            P(("rows", "rep"), None),
        ),
        out_specs=(P(("rows", "rep"), None), P("rep", None, "rows", None), P(), P()),
        check_vma=False,
    )
```

```python
import functools
import math

import jax
import jax.numpy as jnp
from jax import lax
from jax.experimental import pallas as pl
from jax.experimental.pallas import tpu as pltpu
from jax.sharding import PartitionSpec as P

MESH = pl.DeviceIdType.MESH
F32 = jnp.float32
BF16 = jnp.bfloat16
SLOTS = 80
CHUNKS = (4, 1)
KEEP = (32, 16)
VMEM_BYTES = 62 * 2**20
XY_ORDER = (1, 3, 4, 5, 7, 2, 6)


def mm(a, b):
    return lax.dot_general(a, b, (((1,), (0,)), ((), ())), preferred_element_type=F32)


def mm_nt(a, b):
    return lax.dot_general(a, b, (((1,), (1,)), ((), ())), preferred_element_type=F32)


def mm_tn(a, b):
    return lax.dot_general(a, b, (((0,), (0,)), ((), ())), preferred_element_type=F32)


def arrived(ref, sem):
    pltpu.make_async_copy(ref, ref, sem).wait()


def kernel(
    scale,
    feat_hbm, adj_hbm, coord_hbm, count_hbm, w_hbm, b_hbm, cot_hbm,
    hid_hbm, gin_hbm, gw_hbm, gb_hbm,
    coord, count, place, line, tab, adj, feat, acc, pf, ps, pr, rt, acct, xs0, xs1, xr0, xr1, xa, zs, zr, zf, yf, yr,
    w_ref, b_ref, cot_ref, hid_ref, gin_ref, gw_ref, gb_ref, wa_s, wa, wb, wc,
    adj_sem, in_sem, tab_sem, out_sem, s1, s2, s3, r12, r3, ps_s, ps_r, rt_s, rt_r,
    wa_ss, wa_rs, wb_ss, wb_rs, wc_ss, wc_rs,
    xs_s, xs_r, zs_s, zs_r,
    zf_s, zf_r, yf_s, yf_r,
):
    row = lax.axis_index("rows")
    rep = lax.axis_index("rep")
    x = lax.rem(row, 4)
    z = lax.rem(lax.div(row, 4), 8)
    yl = lax.div(row, 32)
    yh = lax.div(rep, 2)
    core = lax.rem(rep, 2)

    def device(x, yl, z, yh, core):
        return (yl * 32 + z * 4 + x, yh * 2 + core)

    def xy_at(k, sign=1):
        return lax.rem(x + sign * (k % 4) + 4, 4), lax.rem(yl + k // 4, 2)

    def xy_peer(k):
        px, pyl = xy_at(k)
        return device(px, pyl, z, yh, core)

    def z_peer(k):
        return device(x, yl, lax.rem(z + k, 8), yh, core)

    def rep_peer(k):
        return device(x, yl, z, lax.rem(yh + k // 2, 2), lax.rem(core + k % 2, 2))

    a_pos = (yh * 2 + yl) * 4 + x
    b_pos = z * 2 + core

    def a_at(k):
        return lax.rem(a_pos + k, 16)

    def a_peer(k):
        pos = a_at(k)
        py = lax.div(pos, 4)
        return device(lax.rem(pos, 4), lax.rem(py, 2), z, lax.div(py, 2), core)

    def b_peer(k):
        pos = lax.rem(b_pos + k, 16)
        return device(x, yl, lax.div(pos, 2), yh, lax.rem(pos, 2))

    def send(src, dst, send_sem, recv_sem, peer):
        return pltpu.make_async_remote_copy(
            src_ref=src, dst_ref=dst, send_sem=send_sem, recv_sem=recv_sem,
            device_id=peer, device_id_type=MESH,
        )

    sent = []

    barrier = pltpu.get_barrier_semaphore()
    greet = [a_peer(k) for k in range(1, 16)]
    greet += [b_peer(k) for k in range(1, 16)]
    for peer in greet:
        pl.semaphore_signal(barrier, inc=1, device_id=peer, device_id_type=MESH)
    part = SLOTS // 4
    for i in range(4):
        pltpu.make_async_copy(
            adj_hbm.at[pl.ds(i * part, part)], adj.at[pl.ds(i * part, part)], adj_sem.at[i]
        ).start()

    small = [(coord_hbm, coord), (count_hbm, count), (w_hbm, w_ref), (b_hbm, b_ref), (cot_hbm, cot_ref)]
    for i, (src, dst) in enumerate(small):
        pltpu.make_async_copy(src, dst, in_sem.at[i]).start()

    pl.semaphore_wait(barrier, len(greet))

    my_j = yl * 4 + x
    is_root = [row == (rep * 2 + s) * 8 for s in range(2)]
    in_plane = [z == core * 4 + s * 2 for s in range(2)]

    def span(s, c):
        size = 256 // CHUNKS[s]
        return pl.ds(c * size, size)

    def root_copy(s, c, k):
        px, pyl = xy_at(k)
        j = pyl * 4 + px
        size = 256 // CHUNKS[s]
        return send(
            feat_hbm.at[pl.ds(pl.multiple_of(j * 256 + c * size, size), size)], feat.at[s, j, span(s, c)],
            s1.at[s, c, k], r12.at[s, c], device(px, pyl, z, yh, core),
        )

    def plane_copy(s, c, k):
        mine = feat.at[s, my_j, span(s, c)]
        return send(mine, mine, s2.at[s, c, k], r12.at[s, c], z_peer(k))

    def side_copy(s, c, k):
        mine = feat.at[s, my_j, span(s, c)]
        return send(mine, mine, s3.at[s, c, k], r3.at[s, c, k], xy_peer(k))

    def drain_if(cond, copy, s):
        @pl.when(cond)
        def _():
            for c in range(CHUNKS[s]):
                for k in range(1, 8):
                    copy(s, c, k).wait_send()

    for s in range(2):
        @pl.when(is_root[s])
        def _():
            for c in range(CHUNKS[s]):
                size = 256 // CHUNKS[s]
                for k in XY_ORDER:
                    root_copy(s, c, k).start()
                pltpu.make_async_copy(
                    feat_hbm.at[pl.ds(pl.multiple_of(my_j * 256 + c * size, size), size)],
                    feat.at[s, my_j, span(s, c)], r12.at[s, c],
                ).start()

        sent.append(functools.partial(drain_if, is_root[s], root_copy, s))

    acc[...] = jnp.zeros_like(acc)
    adj[SLOTS] = jnp.zeros((256, 256), BF16)

    for i, (src, dst) in enumerate(small):
        arrived(dst, in_sem.at[i])
    place[...] = jnp.full((8, 128), -1, jnp.int32)
    slot = lax.broadcasted_iota(jnp.int32, (1, 40), 1)
    for s in range(2):
        where = coord[s, pl.ds(0, 1)] * 8 + coord[s, pl.ds(1, 1)] + s * 64
        place[pl.ds(s, 1), pl.ds(0, 40)] = jnp.where(slot < count[:, s : s + 1], where, -1)
    by_slot = place[...].T
    spot = lax.broadcasted_iota(jnp.int32, (128, 128), 1)
    number = lax.broadcasted_iota(jnp.int32, (128, 128), 0) - SLOTS
    found = jnp.where(by_slot[:, 0:1] == spot, number, 0)
    found += jnp.where(by_slot[:, 1:2] == spot, number + 40, 0)
    line[...] = jnp.sum(found, axis=0, keepdims=True) + SLOTS
    to_scalar = pltpu.make_async_copy(line, tab, tab_sem)
    to_scalar.start()
    to_scalar.wait()

    for s in range(2):
        @pl.when(in_plane[s])
        def _():
            for c in range(CHUNKS[s]):
                arrived(feat.at[s, my_j, span(s, c)], r12.at[s, c])
                for k in (4, 3, 5, 2, 6, 1, 7):
                    plane_copy(s, c, k).start()

        sent.append(functools.partial(drain_if, in_plane[s], plane_copy, s))

    for s in range(2):
        for c in range(CHUNKS[s]):
            @pl.when(jnp.logical_not(in_plane[s]))
            def _():
                arrived(feat.at[s, my_j, span(s, c)], r12.at[s, c])

            for k in XY_ORDER:
                side_copy(s, c, k).start()
                sent.append(side_copy(s, c, k).wait_send)

    for i in range(4):
        view = adj.at[pl.ds(i * part, part)]
        arrived(view, adj_sem.at[i])

    def forward(s, k, carry):
        fx = lax.rem(x - lax.rem(k, 4) + 4, 4)
        fyl = lax.rem(yl + lax.div(k, 4), 2)
        j = fyl * 4 + fx

        @pl.when(k > 0)
        def _():
            for c in range(CHUNKS[s]):
                arrived(feat.at[s, j, span(s, c)], r3.at[s, c, k])

        column = feat[s, j]
        for p in range(8):
            acc[p] += mm(adj[tab[0, s * 64 + p * 8 + j]], column)
        return carry

    for s in range(2):
        lax.fori_loop(0, 8, functools.partial(forward, s), 0, unroll=2)

    far_yh, other = lax.rem(yh + 1, 2), lax.rem(core + 1, 2)

    def core_copy(i):
        quarter = (far_yh, yh)[i // 2] * 2 + other
        return send(acc.at[quarter * 2 + i % 2], pf.at[i // 2, i % 2], ps_s.at[i], ps_r.at[i], rep_peer(1))

    def far_copy(h):
        return send(ps.at[h], pr.at[h], ps_s.at[4 + h], ps_r.at[4 + h], rep_peer(2))

    for i in range(4):
        core_copy(i).start()
        sent.append(core_copy(i).wait_send)
    for h in range(2):
        arrived(pf.at[0, h], ps_r.at[h])
        ps[h] = (acc[(far_yh * 2 + core) * 2 + h] + pf[0, h]).astype(BF16)
        far_copy(h).start()
        sent.append(far_copy(h).wait_send)
    for h in range(2):
        arrived(pf.at[1, h], ps_r.at[2 + h])

    c0 = math.sqrt(2.0 / math.pi)
    weight = w_ref[...]

    def epilogue(h, carry):
        wsum, bsum = carry
        rows = pl.ds(pl.multiple_of(h * 256, 256), 256)
        total = acc[rep * 2 + h] + pf[1, h]
        arrived(pr.at[h], ps_r.at[4 + h])
        total += pr[h].astype(F32)
        agg = total.astype(BF16)
        v = mm(agg, weight) + b_ref[...]
        v2 = v * v
        t = jnp.tanh(c0 * (v + 0.044715 * (v2 * v)))
        half = 0.5 * (1.0 + t)
        hid_ref[rows] = (v * half).astype(BF16)
        slope = half + 0.5 * v * (1.0 - t * t) * (c0 * (1.0 + 0.134145 * v2))
        grad = cot_ref[rows].astype(F32) * slope
        grad_bf = grad.astype(BF16)
        rt[rep, :, rows] = mm_nt(weight, grad_bf).astype(BF16)
        wsum = wsum + mm_tn(agg, grad_bf)
        bsum = bsum + jnp.sum(grad.reshape(32, 8, 256), axis=0)
        return wsum, bsum

    carry = (jnp.zeros((128, 256), F32), jnp.zeros((8, 256), F32))
    for h in range(2):
        carry = epilogue(h, carry)
    wsum, bsum = carry

    def put(i, src, dst):
        copy = pltpu.make_async_copy(src, dst, out_sem.at[i])
        copy.start()
        sent.append(copy.wait)

    def rows_copy(k):
        return send(rt.at[rep], rt.at[rep], rt_s.at[k], rt_r.at[k], rep_peer(k))

    def pass_on():
        far = rt.at[lax.rem(yh + 1, 2) * 2 + core]
        return send(far, far, rt_s.at[3], rt_r.at[3], rep_peer(1))

    for k in (2, 1):
        rows_copy(k).start()
        sent.append(rows_copy(k).wait_send)

    put(0, hid_ref, hid_hbm)

    for j in range(16):
        for h in range(2):
            wa_s[j, pl.ds(h * 8, 8)] = wsum[j * 8 : j * 8 + 8, h * 128 : h * 128 + 128]
        wa_s[j, pl.ds(16, 8)] = bsum[:, (j % 2) * 128 : (j % 2) * 128 + 128]

    def wa_copy(k):
        return send(wa_s.at[a_at(k)], wa.at[a_pos], wa_ss.at[k], wa_rs.at[k], a_peer(k))

    for k in range(1, 16):
        wa_copy(k).start()
        sent.append(wa_copy(k).wait_send)
    wa[a_pos] = wa_s[a_pos]

    def wb_copy(k):
        return send(wb.at[b_pos], wb.at[b_pos], wb_ss.at[k], wb_rs.at[k], b_peer(k))

    def add_up(ref):
        total = ref[0]
        for j in range(1, 16):
            total = total + ref[j]
        return total

    def step_b():
        for k in range(1, 16):
            arrived(wa.at[lax.rem(a_pos - k + 16, 16)], wa_rs.at[k])
        wb[b_pos] = add_up(wa)
        for k in range(1, 16):
            wb_copy(k).start()
            sent.append(wb_copy(k).wait_send)

    def wc_copy(k):
        return send(wc.at[a_pos], wc.at[a_pos], wc_ss.at[k], wc_rs.at[k], a_peer(k))

    def step_c():
        for k in range(1, 16):
            arrived(wb.at[lax.rem(b_pos - k + 16, 16)], wb_rs.at[k])
        wc[a_pos] = add_up(wb) * scale
        for k in range(1, 16):
            wc_copy(k).start()
            sent.append(wc_copy(k).wait_send)

    def quarter_of(k):
        return lax.rem(yh + k // 2, 2) * 2 + lax.rem(core + k % 2, 2)

    def back_terms(s, q, quarter):
        left = rt[quarter]
        out = mm(left[:, :256], adj[tab[0, s * 64 + quarter * 16 + q]])
        return out + mm(left[:, 256:], adj[tab[0, s * 64 + quarter * 16 + 8 + q]])

    def back_own(i, carry):
        s, q = lax.div(i, 8), lax.rem(i, 8)
        acct[s, q] = back_terms(s, q, quarter_of(0))
        return carry

    lax.fori_loop(0, 16, back_own, 0, unroll=4)
    arrived(rt.at[quarter_of(1)], rt_r.at[1])

    def back_core(i, carry):
        s, q = lax.div(i, 8), lax.rem(i, 8)
        acct[s, q] += back_terms(s, q, quarter_of(1))
        return carry

    lax.fori_loop(0, 16, back_core, 0, unroll=4)
    arrived(rt.at[quarter_of(2)], rt_r.at[2])
    pass_on().start()
    sent.append(pass_on().wait_send)

    def back_far(i, carry):
        s, q = lax.div(i, 8), lax.rem(i, 8)
        acct[s, q] += back_terms(s, q, quarter_of(2))
        return carry

    step_b()
    lax.fori_loop(0, 16, back_far, 0, unroll=4)
    arrived(rt.at[quarter_of(3)], rt_r.at[3])

    xs, xr = (xs0, xs1), (xr0, xr1)

    def xs_copy(s, k):
        px, pyl = xy_at(k)
        return send(xs[s].at[pyl * 4 + px], xr[s].at[k], xs_s.at[s, k], xs_r.at[s, k], xy_peer(k))

    late = pl.ds(KEEP[1], 32 - KEEP[1])

    def zf_copy(k):
        return send(xa.at[lax.rem(z + k, 8)], zf.at[k], zf_s.at[k], zf_r.at[k], z_peer(k))

    def yf_copy(k):
        px, pyl = xy_at(k)
        return send(yf.at[pyl * 4 + px], yr.at[k], yf_s.at[k], yf_r.at[k], xy_peer(k))

    for s in range(2):
        for hk in (1, 0):
            half = lax.rem(yl + hk, 2)

            def back_rest(zz, carry):
                q = half * 4 + zz
                total = acct[s, q] + back_terms(s, q, quarter_of(3))
                out = total.T.astype(BF16)
                for zl in range(2):
                    for px in range(4):
                        at = zl * 128 + px * 32
                        keep = KEEP[s]
                        xs[s][half * 4 + px, zz * 2 + zl] = out[at : at + keep]
                        if s == 1:
                            xa[zz * 2 + zl, half * 4 + px] = out[at + keep : at + 32]
                return carry

            lax.fori_loop(0, 4, back_rest, 0, unroll=True)
            for k in (1, 3, 2) if hk == 0 else (4, 5, 7, 6):
                xs_copy(s, k).start()
                sent.append(xs_copy(s, k).wait_send)
    for k in (4, 3, 5, 2, 6, 1, 7):
        zf_copy(k).start()
        sent.append(zf_copy(k).wait_send)

    step_c()

    def zs_copy(s, k):
        rows = pl.ds(0, KEEP[s])
        return send(
            zs.at[s, lax.rem(z + k, 8), rows], zr.at[s, k, rows], zs_s.at[s, k], zs_r.at[s, k], z_peer(k)
        )

    def over_xy(s):
        rows = pl.ds(0, KEEP[s])
        for k in range(1, 8):
            arrived(xr[s].at[k], xs_r.at[s, k])
        for zz in range(8):
            total = xs[s][my_j, zz].astype(F32)
            for k in range(1, 8):
                total += xr[s][k, zz].astype(F32)
            zs[s, zz, rows] = total.astype(BF16)
        for k in (4, 3, 5, 2, 6, 1, 7):
            zs_copy(s, k).start()
            sent.append(zs_copy(s, k).wait_send)

    over_xy(0)
    for k in range(1, 8):
        arrived(zf.at[k], zf_r.at[k])
    for j in range(8):
        total = xa[z, j].astype(F32)
        for k in range(1, 8):
            total += zf[k, j].astype(F32)
        yf[j] = total.astype(BF16)
    for k in XY_ORDER:
        yf_copy(k).start()
        sent.append(yf_copy(k).wait_send)
    over_xy(1)

    for s in range(2):
        rows = pl.ds(0, KEEP[s])
        total = zs[s, z, rows].astype(F32)
        for k in range(1, 8):
            arrived(zr.at[s, k, rows], zs_r.at[s, k])
            total += zr[s, k, rows].astype(F32)
        gin_ref[s, rows] = total.astype(BF16)
    total = yf[my_j].astype(F32)
    for k in range(1, 8):
        arrived(yr.at[k], yf_r.at[k])
        total += yr[k].astype(F32)
    gin_ref[1, late] = total.astype(BF16)
    put(1, gin_ref, gin_hbm)

    for k in range(1, 16):
        arrived(wc.at[lax.rem(a_pos - k + 16, 16)], wc_rs.at[k])
    for j in range(16):
        for h in range(2):
            gw_ref[j, :, pl.ds(h * 128, 128)] = wc[j, pl.ds(h * 8, 8)]
    for h in range(2):
        gb_ref[:, pl.ds(h * 128, 128)] = jnp.sum(wc[h, pl.ds(16, 8)], axis=0, keepdims=True)
    put(2, gw_ref, gw_hbm)
    put(3, gb_ref, gb_hbm)

    for drain in sent:
        drain()


def layer(features, adjacency, coords, counts, weight, bias, cotangent, scale):
    hbm = pl.BlockSpec(memory_space=pltpu.HBM)
    sems = [
        (4,), (5,), (), (4,), (2, 4, 8), (2, 4, 8), (2, 4, 8), (2, 4), (2, 4, 8), (8,), (8,), (4,), (4,),
        (16,), (16,), (16,), (16,), (16,), (16,),
        (2, 8), (2, 8), (2, 8), (2, 8), (8,), (8,), (8,), (8,),
    ]
    return pl.pallas_call(
        functools.partial(kernel, scale),
        name="layer",
        out_shape=(
            jax.ShapeDtypeStruct((512, 256), BF16),
            jax.ShapeDtypeStruct((2, 32, 128), BF16),
            jax.ShapeDtypeStruct((16, 8, 256), F32),
            jax.ShapeDtypeStruct((1, 256), F32),
        ),
        in_specs=[hbm] * 7,
        out_specs=(hbm, hbm, hbm, hbm),
        scratch_shapes=[
            pltpu.VMEM((2, 2, 40), jnp.int32),
            pltpu.VMEM((1, 2), jnp.int32),
            pltpu.VMEM((8, 128), jnp.int32),
            pltpu.VMEM((1, 128), jnp.int32),
            pltpu.SMEM((1, 128), jnp.int32),
            pltpu.VMEM((SLOTS + 1, 256, 256), BF16),
            pltpu.VMEM((2, 8, 256, 128), BF16),
            pltpu.VMEM((8, 256, 128), F32),
            pltpu.VMEM((2, 2, 256, 128), F32),
            pltpu.VMEM((2, 256, 128), BF16),
            pltpu.VMEM((2, 256, 128), BF16),
            pltpu.VMEM((4, 128, 512), BF16),
            pltpu.VMEM((2, 8, 128, 256), F32),
            pltpu.VMEM((8, 8, KEEP[0], 128), BF16),
            pltpu.VMEM((8, 8, KEEP[1], 128), BF16),
            pltpu.VMEM((8, 8, KEEP[0], 128), BF16),
            pltpu.VMEM((8, 8, KEEP[1], 128), BF16),
            pltpu.VMEM((8, 8, 32 - KEEP[1], 128), BF16),
            pltpu.VMEM((2, 8, 32, 128), BF16),
            pltpu.VMEM((2, 8, 32, 128), BF16),
            pltpu.VMEM((8, 8, 16, 128), BF16),
            pltpu.VMEM((8, 16, 128), BF16),
            pltpu.VMEM((8, 16, 128), BF16),
            pltpu.VMEM((128, 256), BF16),
            pltpu.VMEM((1, 256), F32),
            pltpu.VMEM((512, 256), BF16),
            pltpu.VMEM((512, 256), BF16),
            pltpu.VMEM((2, 32, 128), BF16),
            pltpu.VMEM((16, 8, 256), F32),
            pltpu.VMEM((1, 256), F32),
            pltpu.VMEM((16, 24, 128), F32),
            pltpu.VMEM((16, 24, 128), F32),
            pltpu.VMEM((16, 24, 128), F32),
            pltpu.VMEM((16, 24, 128), F32),
        ]
        + [pltpu.SemaphoreType.DMA(shape) for shape in sems],
        compiler_params=pltpu.CompilerParams(
            collective_id=1, has_side_effects=True, vmem_limit_bytes=VMEM_BYTES
        ),
    )(features, adjacency, coords, counts, weight, bias, cotangent)


def finish_kernel(n, *refs):
    ins, outs, held, sem = refs[:n], refs[n : 2 * n], refs[2 * n : 3 * n], refs[3 * n]
    loads = [pltpu.make_async_copy(ins[i], held[i], sem.at[0, i]) for i in range(n)]
    stores = [pltpu.make_async_copy(held[i], outs[i], sem.at[1, i]) for i in range(n)]
    for copy in loads:
        copy.start()
    for load, store in zip(loads, stores):
        load.wait()
        store.start()
    for copy in stores:
        copy.wait()


def finish(*arrays):
    n = len(arrays)
    hbm = pl.BlockSpec(memory_space=pltpu.HBM)
    return pl.pallas_call(
        functools.partial(finish_kernel, n),
        name="finish",
        out_shape=tuple(jax.ShapeDtypeStruct(a.shape, a.dtype) for a in arrays),
        in_specs=[hbm] * n,
        out_specs=(hbm,) * n,
        scratch_shapes=[pltpu.VMEM(a.shape, a.dtype) for a in arrays]
        + [pltpu.SemaphoreType.DMA((2, n))],
        compiler_params=pltpu.CompilerParams(vmem_limit_bytes=VMEM_BYTES),
    )(*arrays)


def shards(features, adjacency, tile_coords, tile_counts, weight, bias, cotangent):
    rows_count = lax.axis_size("rows")
    scale = 1.0 / math.sqrt(features.shape[0] * rows_count)
    hidden, grad_inputs, grad_weight, grad_bias = layer(
        features,
        adjacency.reshape(SLOTS, 256, 256),
        tile_coords.reshape(2, 2, 40),
        tile_counts.reshape(1, 2),
        weight,
        bias.reshape(1, 256),
        cotangent,
        scale,
    )
    hidden, grad_inputs, grad_weight, grad_bias = finish(
        hidden, grad_inputs, grad_weight, grad_bias
    )
    return hidden, grad_inputs[None], grad_weight.reshape(128, 256), grad_bias.reshape(256)


def solution(mesh):
    return jax.shard_map(
        shards,
        mesh=mesh,
        in_specs=(
            P("rows", None),
            P("rows", "rep", None, None, None, None),
            P("rows", "rep", None, None, None),
            P("rows", "rep", None),
            P(),
            P(),
            P(("rows", "rep"), None),
        ),
        out_specs=(P(("rows", "rep"), None), P("rep", None, "rows", None), P(), P()),
        check_vma=False,
    )
```

```python
import functools
import math

import jax
import jax.numpy as jnp
from jax import lax
from jax.experimental import pallas as pl
from jax.experimental.pallas import tpu as pltpu
from jax.sharding import PartitionSpec as P

MESH = pl.DeviceIdType.MESH
F32 = jnp.float32
BF16 = jnp.bfloat16
SLOTS = 80
CHUNKS = (4, 1)
KEEP = (32, 16)
VMEM_BYTES = 62 * 2**20
XY_ORDER = (1, 3, 4, 5, 7, 2, 6)


def mm(a, b):
    return lax.dot_general(a, b, (((1,), (0,)), ((), ())), preferred_element_type=F32)


def mm_nt(a, b):
    return lax.dot_general(a, b, (((1,), (1,)), ((), ())), preferred_element_type=F32)


def mm_tn(a, b):
    return lax.dot_general(a, b, (((0,), (0,)), ((), ())), preferred_element_type=F32)


def arrived(ref, sem):
    pltpu.make_async_copy(ref, ref, sem).wait()


def kernel(
    scale,
    feat_hbm, adj_hbm, coord_hbm, count_hbm, w_hbm, b_hbm, cot_hbm,
    hid_hbm, gin_hbm, gw_hbm, gb_hbm,
    coord, count, place, line, tab, adj, feat, acc, pf, ps, pr, rt, acct, xs0, xs1, xr0, xr1, xa, zs, zr, zf, yf, yr,
    w_ref, b_ref, cot_ref, hid_ref, gin_ref, gw_ref, gb_ref, wa_s, wa, wb, wc,
    adj_sem, in_sem, tab_sem, out_sem, s1, s2, s3, r12, r3, ps_s, ps_r, rt_s, rt_r,
    wa_ss, wa_rs, wb_ss, wb_rs, wc_ss, wc_rs,
    xs_s, xs_r, zs_s, zs_r,
    zf_s, zf_r, yf_s, yf_r,
):
    row = lax.axis_index("rows")
    rep = lax.axis_index("rep")
    x = lax.rem(row, 4)
    z = lax.rem(lax.div(row, 4), 8)
    yl = lax.div(row, 32)
    yh = lax.div(rep, 2)
    core = lax.rem(rep, 2)

    def device(x, yl, z, yh, core):
        return (yl * 32 + z * 4 + x, yh * 2 + core)

    def xy_at(k, sign=1):
        return lax.rem(x + sign * (k % 4) + 4, 4), lax.rem(yl + k // 4, 2)

    def xy_peer(k):
        px, pyl = xy_at(k)
        return device(px, pyl, z, yh, core)

    def z_peer(k):
        return device(x, yl, lax.rem(z + k, 8), yh, core)

    def rep_peer(k):
        return device(x, yl, z, lax.rem(yh + k // 2, 2), lax.rem(core + k % 2, 2))

    a_pos = (yh * 2 + yl) * 4 + x
    b_pos = z * 2 + core

    def a_at(k):
        return lax.rem(a_pos + k, 16)

    def a_peer(k):
        pos = a_at(k)
        py = lax.div(pos, 4)
        return device(lax.rem(pos, 4), lax.rem(py, 2), z, lax.div(py, 2), core)

    def b_peer(k):
        pos = lax.rem(b_pos + k, 16)
        return device(x, yl, lax.div(pos, 2), yh, lax.rem(pos, 2))

    def send(src, dst, send_sem, recv_sem, peer):
        return pltpu.make_async_remote_copy(
            src_ref=src, dst_ref=dst, send_sem=send_sem, recv_sem=recv_sem,
            device_id=peer, device_id_type=MESH,
        )

    sent = []

    barrier = pltpu.get_barrier_semaphore()
    greet = [a_peer(k) for k in range(1, 16)]
    greet += [b_peer(k) for k in range(1, 16)]
    for peer in greet:
        pl.semaphore_signal(barrier, inc=1, device_id=peer, device_id_type=MESH)
    part = SLOTS // 4
    for i in range(4):
        pltpu.make_async_copy(
            adj_hbm.at[pl.ds(i * part, part)], adj.at[pl.ds(i * part, part)], adj_sem.at[i]
        ).start()

    small = [(coord_hbm, coord), (count_hbm, count), (w_hbm, w_ref), (b_hbm, b_ref), (cot_hbm, cot_ref)]
    for i, (src, dst) in enumerate(small):
        pltpu.make_async_copy(src, dst, in_sem.at[i]).start()

    pl.semaphore_wait(barrier, len(greet))

    my_j = yl * 4 + x
    is_root = [row == (rep * 2 + s) * 8 for s in range(2)]
    in_plane = [z == core * 4 + s * 2 for s in range(2)]

    def span(s, c):
        size = 256 // CHUNKS[s]
        return pl.ds(c * size, size)

    def root_copy(s, c, k):
        px, pyl = xy_at(k)
        j = pyl * 4 + px
        size = 256 // CHUNKS[s]
        return send(
            feat_hbm.at[pl.ds(pl.multiple_of(j * 256 + c * size, size), size)], feat.at[s, j, span(s, c)],
            s1.at[s, c, k], r12.at[s, c], device(px, pyl, z, yh, core),
        )

    def plane_copy(s, c, k):
        mine = feat.at[s, my_j, span(s, c)]
        return send(mine, mine, s2.at[s, c, k], r12.at[s, c], z_peer(k))

    def side_copy(s, c, k):
        mine = feat.at[s, my_j, span(s, c)]
        return send(mine, mine, s3.at[s, c, k], r3.at[s, c, k], xy_peer(k))

    def drain_if(cond, copy, s):
        @pl.when(cond)
        def _():
            for c in range(CHUNKS[s]):
                for k in range(1, 8):
                    copy(s, c, k).wait_send()

    for s in range(2):
        @pl.when(is_root[s])
        def _():
            for c in range(CHUNKS[s]):
                size = 256 // CHUNKS[s]
                for k in XY_ORDER:
                    root_copy(s, c, k).start()
                pltpu.make_async_copy(
                    feat_hbm.at[pl.ds(pl.multiple_of(my_j * 256 + c * size, size), size)],
                    feat.at[s, my_j, span(s, c)], r12.at[s, c],
                ).start()

        sent.append(functools.partial(drain_if, is_root[s], root_copy, s))

    acc[...] = jnp.zeros_like(acc)
    adj[SLOTS] = jnp.zeros((256, 256), BF16)

    for i, (src, dst) in enumerate(small):
        arrived(dst, in_sem.at[i])
    place[...] = jnp.full((8, 128), -1, jnp.int32)
    slot = lax.broadcasted_iota(jnp.int32, (1, 40), 1)
    for s in range(2):
        where = coord[s, pl.ds(0, 1)] * 8 + coord[s, pl.ds(1, 1)] + s * 64
        place[pl.ds(s, 1), pl.ds(0, 40)] = jnp.where(slot < count[:, s : s + 1], where, -1)
    by_slot = place[...].T
    spot = lax.broadcasted_iota(jnp.int32, (128, 128), 1)
    number = lax.broadcasted_iota(jnp.int32, (128, 128), 0) - SLOTS
    found = jnp.where(by_slot[:, 0:1] == spot, number, 0)
    found += jnp.where(by_slot[:, 1:2] == spot, number + 40, 0)
    line[...] = jnp.sum(found, axis=0, keepdims=True) + SLOTS
    to_scalar = pltpu.make_async_copy(line, tab, tab_sem)
    to_scalar.start()
    to_scalar.wait()

    for s in range(2):
        @pl.when(in_plane[s])
        def _():
            for c in range(CHUNKS[s]):
                arrived(feat.at[s, my_j, span(s, c)], r12.at[s, c])
                for k in (4, 3, 5, 2, 6, 1, 7):
                    plane_copy(s, c, k).start()

        sent.append(functools.partial(drain_if, in_plane[s], plane_copy, s))

    for s in range(2):
        for c in range(CHUNKS[s]):
            @pl.when(jnp.logical_not(in_plane[s]))
            def _():
                arrived(feat.at[s, my_j, span(s, c)], r12.at[s, c])

            for k in XY_ORDER:
                side_copy(s, c, k).start()
                sent.append(side_copy(s, c, k).wait_send)

    for i in range(4):
        view = adj.at[pl.ds(i * part, part)]
        arrived(view, adj_sem.at[i])

    def forward(s, k, carry):
        fx = lax.rem(x - lax.rem(k, 4) + 4, 4)
        fyl = lax.rem(yl + lax.div(k, 4), 2)
        j = fyl * 4 + fx

        @pl.when(k > 0)
        def _():
            for c in range(CHUNKS[s]):
                arrived(feat.at[s, j, span(s, c)], r3.at[s, c, k])

        column = feat[s, j]
        for p in range(8):
            acc[p] += mm(adj[tab[0, s * 64 + p * 8 + j]], column)
        return carry

    for s in range(2):
        lax.fori_loop(0, 8, functools.partial(forward, s), 0, unroll=2)

    far_yh, other = lax.rem(yh + 1, 2), lax.rem(core + 1, 2)

    def core_copy(i):
        quarter = (far_yh, yh)[i // 2] * 2 + other
        return send(acc.at[quarter * 2 + i % 2], pf.at[i // 2, i % 2], ps_s.at[i], ps_r.at[i], rep_peer(1))

    def far_copy(h):
        return send(ps.at[h], pr.at[h], ps_s.at[4 + h], ps_r.at[4 + h], rep_peer(2))

    for i in range(4):
        core_copy(i).start()
        sent.append(core_copy(i).wait_send)
    for h in range(2):
        arrived(pf.at[0, h], ps_r.at[h])
        ps[h] = (acc[(far_yh * 2 + core) * 2 + h] + pf[0, h]).astype(BF16)
        far_copy(h).start()
        sent.append(far_copy(h).wait_send)
    for h in range(2):
        arrived(pf.at[1, h], ps_r.at[2 + h])

    c0 = math.sqrt(2.0 / math.pi)
    weight = w_ref[...]

    def far_rows(h):
        return send(rt.at[rep, h], rt.at[rep, h], rt_s.at[h], rt_r.at[h], rep_peer(2))

    def pass_on(h):
        far = rt.at[lax.rem(yh + 1, 2) * 2 + core, h]
        return send(far, far, rt_s.at[2 + h], rt_r.at[2 + h], rep_peer(1))

    def near_rows():
        return send(rt.at[rep], rt.at[rep], rt_s.at[4], rt_r.at[4], rep_peer(1))

    def epilogue(h, carry):
        wsum, bsum = carry
        rows = pl.ds(pl.multiple_of(h * 256, 256), 256)
        total = acc[rep * 2 + h] + pf[1, h]
        arrived(pr.at[h], ps_r.at[4 + h])
        total += pr[h].astype(F32)
        agg = total.astype(BF16)
        v = mm(agg, weight) + b_ref[...]
        v2 = v * v
        t = jnp.tanh(c0 * (v + 0.044715 * (v2 * v)))
        half = 0.5 * (1.0 + t)
        hid_ref[rows] = (v * half).astype(BF16)
        slope = half + 0.5 * v * (1.0 - t * t) * (c0 * (1.0 + 0.134145 * v2))
        grad = cot_ref[rows].astype(F32) * slope
        grad_bf = grad.astype(BF16)
        rt[rep, h] = mm_nt(weight, grad_bf).astype(BF16)
        far_rows(h).start()
        sent.append(far_rows(h).wait_send)
        wsum = wsum + mm_tn(agg, grad_bf)
        bsum = bsum + jnp.sum(grad.reshape(32, 8, 256), axis=0)
        return wsum, bsum

    carry = (jnp.zeros((128, 256), F32), jnp.zeros((8, 256), F32))
    for h in range(2):
        carry = epilogue(h, carry)
    wsum, bsum = carry

    def put(i, src, dst):
        copy = pltpu.make_async_copy(src, dst, out_sem.at[i])
        copy.start()
        sent.append(copy.wait)

    near_rows().start()
    sent.append(near_rows().wait_send)

    put(0, hid_ref, hid_hbm)

    for j in range(16):
        for h in range(2):
            wa_s[j, pl.ds(h * 8, 8)] = wsum[j * 8 : j * 8 + 8, h * 128 : h * 128 + 128]
        wa_s[j, pl.ds(16, 8)] = bsum[:, (j % 2) * 128 : (j % 2) * 128 + 128]

    def wa_copy(k):
        return send(wa_s.at[a_at(k)], wa.at[a_pos], wa_ss.at[k], wa_rs.at[k], a_peer(k))

    for k in range(1, 16):
        wa_copy(k).start()
        sent.append(wa_copy(k).wait_send)
    wa[a_pos] = wa_s[a_pos]

    def wb_copy(k):
        return send(wb.at[b_pos], wb.at[b_pos], wb_ss.at[k], wb_rs.at[k], b_peer(k))

    def add_up(ref):
        total = ref[0]
        for j in range(1, 16):
            total = total + ref[j]
        return total

    def step_b():
        for k in range(1, 16):
            arrived(wa.at[lax.rem(a_pos - k + 16, 16)], wa_rs.at[k])
        wb[b_pos] = add_up(wa)
        for k in range(1, 16):
            wb_copy(k).start()
            sent.append(wb_copy(k).wait_send)

    def wc_copy(k):
        return send(wc.at[a_pos], wc.at[a_pos], wc_ss.at[k], wc_rs.at[k], a_peer(k))

    def step_c():
        for k in range(1, 16):
            arrived(wb.at[lax.rem(b_pos - k + 16, 16)], wb_rs.at[k])
        wc[a_pos] = add_up(wb) * scale
        for k in range(1, 16):
            wc_copy(k).start()
            sent.append(wc_copy(k).wait_send)

    def quarter_of(k):
        return lax.rem(yh + k // 2, 2) * 2 + lax.rem(core + k % 2, 2)

    def back_term(s, q, quarter, h):
        return mm(rt[quarter, h], adj[tab[0, s * 64 + quarter * 16 + h * 8 + q]])

    def back_terms(s, q, quarter):
        return back_term(s, q, quarter, 0) + back_term(s, q, quarter, 1)

    def back_own(i, carry):
        s, q = lax.div(i, 8), lax.rem(i, 8)
        acct[s, q] = back_terms(s, q, quarter_of(0))
        return carry

    lax.fori_loop(0, 16, back_own, 0, unroll=4)
    arrived(rt.at[quarter_of(1)], rt_r.at[4])

    def back_core(i, carry):
        s, q = lax.div(i, 8), lax.rem(i, 8)
        acct[s, q] += back_terms(s, q, quarter_of(1))
        return carry

    lax.fori_loop(0, 16, back_core, 0, unroll=4)
    def back_far(h, i, carry):
        s, q = lax.div(i, 8), lax.rem(i, 8)
        acct[s, q] += back_term(s, q, quarter_of(2), h)
        return carry

    for h in range(2):
        arrived(rt.at[quarter_of(2), h], rt_r.at[h])
        pass_on(h).start()
        sent.append(pass_on(h).wait_send)
        if h == 1:
            step_b()
        lax.fori_loop(0, 16, functools.partial(back_far, h), 0, unroll=4)
    for h in range(2):
        arrived(rt.at[quarter_of(3), h], rt_r.at[2 + h])

    xs, xr = (xs0, xs1), (xr0, xr1)

    def xs_copy(s, k):
        px, pyl = xy_at(k)
        return send(xs[s].at[pyl * 4 + px], xr[s].at[k], xs_s.at[s, k], xs_r.at[s, k], xy_peer(k))

    late = pl.ds(KEEP[1], 32 - KEEP[1])

    def zf_copy(k):
        return send(xa.at[lax.rem(z + k, 8)], zf.at[k], zf_s.at[k], zf_r.at[k], z_peer(k))

    def yf_copy(k):
        px, pyl = xy_at(k)
        return send(yf.at[pyl * 4 + px], yr.at[k], yf_s.at[k], yf_r.at[k], xy_peer(k))

    for s in range(2):
        for hk in (1, 0):
            half = lax.rem(yl + hk, 2)

            def back_rest(zz, carry):
                q = half * 4 + zz
                total = acct[s, q] + back_terms(s, q, quarter_of(3))
                out = total.T.astype(BF16)
                for zl in range(2):
                    for px in range(4):
                        at = zl * 128 + px * 32
                        keep = KEEP[s]
                        xs[s][half * 4 + px, zz * 2 + zl] = out[at : at + keep]
                        if s == 1:
                            xa[zz * 2 + zl, half * 4 + px] = out[at + keep : at + 32]
                return carry

            lax.fori_loop(0, 4, back_rest, 0, unroll=True)
            for k in (1, 3, 2) if hk == 0 else (4, 5, 7, 6):
                xs_copy(s, k).start()
                sent.append(xs_copy(s, k).wait_send)
    for k in (4, 3, 5, 2, 6, 1, 7):
        zf_copy(k).start()
        sent.append(zf_copy(k).wait_send)

    step_c()

    def zs_copy(s, k):
        rows = pl.ds(0, KEEP[s])
        return send(
            zs.at[s, lax.rem(z + k, 8), rows], zr.at[s, k, rows], zs_s.at[s, k], zs_r.at[s, k], z_peer(k)
        )

    def over_xy(s):
        rows = pl.ds(0, KEEP[s])
        for k in range(1, 8):
            arrived(xr[s].at[k], xs_r.at[s, k])
        for zz in range(8):
            total = xs[s][my_j, zz].astype(F32)
            for k in range(1, 8):
                total += xr[s][k, zz].astype(F32)
            zs[s, zz, rows] = total.astype(BF16)
        for k in (4, 3, 5, 2, 6, 1, 7):
            zs_copy(s, k).start()
            sent.append(zs_copy(s, k).wait_send)

    over_xy(0)
    for k in range(1, 8):
        arrived(zf.at[k], zf_r.at[k])
    for j in range(8):
        total = xa[z, j].astype(F32)
        for k in range(1, 8):
            total += zf[k, j].astype(F32)
        yf[j] = total.astype(BF16)
    for k in XY_ORDER:
        yf_copy(k).start()
        sent.append(yf_copy(k).wait_send)
    over_xy(1)

    for s in range(2):
        rows = pl.ds(0, KEEP[s])
        total = zs[s, z, rows].astype(F32)
        for k in range(1, 8):
            arrived(zr.at[s, k, rows], zs_r.at[s, k])
            total += zr[s, k, rows].astype(F32)
        gin_ref[s, rows] = total.astype(BF16)
    total = yf[my_j].astype(F32)
    for k in range(1, 8):
        arrived(yr.at[k], yf_r.at[k])
        total += yr[k].astype(F32)
    gin_ref[1, late] = total.astype(BF16)
    put(1, gin_ref, gin_hbm)

    for k in range(1, 16):
        arrived(wc.at[lax.rem(a_pos - k + 16, 16)], wc_rs.at[k])
    for j in range(16):
        for h in range(2):
            gw_ref[j, :, pl.ds(h * 128, 128)] = wc[j, pl.ds(h * 8, 8)]
    for h in range(2):
        gb_ref[:, pl.ds(h * 128, 128)] = jnp.sum(wc[h, pl.ds(16, 8)], axis=0, keepdims=True)
    put(2, gw_ref, gw_hbm)
    put(3, gb_ref, gb_hbm)

    for drain in sent:
        drain()


def layer(features, adjacency, coords, counts, weight, bias, cotangent, scale):
    hbm = pl.BlockSpec(memory_space=pltpu.HBM)
    sems = [
        (4,), (5,), (), (4,), (2, 4, 8), (2, 4, 8), (2, 4, 8), (2, 4), (2, 4, 8), (8,), (8,), (8,), (8,),
        (16,), (16,), (16,), (16,), (16,), (16,),
        (2, 8), (2, 8), (2, 8), (2, 8), (8,), (8,), (8,), (8,),
    ]
    return pl.pallas_call(
        functools.partial(kernel, scale),
        name="layer",
        out_shape=(
            jax.ShapeDtypeStruct((512, 256), BF16),
            jax.ShapeDtypeStruct((2, 32, 128), BF16),
            jax.ShapeDtypeStruct((16, 8, 256), F32),
            jax.ShapeDtypeStruct((1, 256), F32),
        ),
        in_specs=[hbm] * 7,
        out_specs=(hbm, hbm, hbm, hbm),
        scratch_shapes=[
            pltpu.VMEM((2, 2, 40), jnp.int32),
            pltpu.VMEM((1, 2), jnp.int32),
            pltpu.VMEM((8, 128), jnp.int32),
            pltpu.VMEM((1, 128), jnp.int32),
            pltpu.SMEM((1, 128), jnp.int32),
            pltpu.VMEM((SLOTS + 1, 256, 256), BF16),
            pltpu.VMEM((2, 8, 256, 128), BF16),
            pltpu.VMEM((8, 256, 128), F32),
            pltpu.VMEM((2, 2, 256, 128), F32),
            pltpu.VMEM((2, 256, 128), BF16),
            pltpu.VMEM((2, 256, 128), BF16),
            pltpu.VMEM((4, 2, 128, 256), BF16),
            pltpu.VMEM((2, 8, 128, 256), F32),
            pltpu.VMEM((8, 8, KEEP[0], 128), BF16),
            pltpu.VMEM((8, 8, KEEP[1], 128), BF16),
            pltpu.VMEM((8, 8, KEEP[0], 128), BF16),
            pltpu.VMEM((8, 8, KEEP[1], 128), BF16),
            pltpu.VMEM((8, 8, 32 - KEEP[1], 128), BF16),
            pltpu.VMEM((2, 8, 32, 128), BF16),
            pltpu.VMEM((2, 8, 32, 128), BF16),
            pltpu.VMEM((8, 8, 16, 128), BF16),
            pltpu.VMEM((8, 16, 128), BF16),
            pltpu.VMEM((8, 16, 128), BF16),
            pltpu.VMEM((128, 256), BF16),
            pltpu.VMEM((1, 256), F32),
            pltpu.VMEM((512, 256), BF16),
            pltpu.VMEM((512, 256), BF16),
            pltpu.VMEM((2, 32, 128), BF16),
            pltpu.VMEM((16, 8, 256), F32),
            pltpu.VMEM((1, 256), F32),
            pltpu.VMEM((16, 24, 128), F32),
            pltpu.VMEM((16, 24, 128), F32),
            pltpu.VMEM((16, 24, 128), F32),
            pltpu.VMEM((16, 24, 128), F32),
        ]
        + [pltpu.SemaphoreType.DMA(shape) for shape in sems],
        compiler_params=pltpu.CompilerParams(
            collective_id=1, has_side_effects=True, vmem_limit_bytes=VMEM_BYTES
        ),
    )(features, adjacency, coords, counts, weight, bias, cotangent)


def finish_kernel(n, *refs):
    ins, outs, held, sem = refs[:n], refs[n : 2 * n], refs[2 * n : 3 * n], refs[3 * n]
    loads = [pltpu.make_async_copy(ins[i], held[i], sem.at[0, i]) for i in range(n)]
    stores = [pltpu.make_async_copy(held[i], outs[i], sem.at[1, i]) for i in range(n)]
    for copy in loads:
        copy.start()
    for load, store in zip(loads, stores):
        load.wait()
        store.start()
    for copy in stores:
        copy.wait()


def finish(*arrays):
    n = len(arrays)
    hbm = pl.BlockSpec(memory_space=pltpu.HBM)
    return pl.pallas_call(
        functools.partial(finish_kernel, n),
        name="finish",
        out_shape=tuple(jax.ShapeDtypeStruct(a.shape, a.dtype) for a in arrays),
        in_specs=[hbm] * n,
        out_specs=(hbm,) * n,
        scratch_shapes=[pltpu.VMEM(a.shape, a.dtype) for a in arrays]
        + [pltpu.SemaphoreType.DMA((2, n))],
        compiler_params=pltpu.CompilerParams(vmem_limit_bytes=VMEM_BYTES),
    )(*arrays)


def shards(features, adjacency, tile_coords, tile_counts, weight, bias, cotangent):
    rows_count = lax.axis_size("rows")
    scale = 1.0 / math.sqrt(features.shape[0] * rows_count)
    hidden, grad_inputs, grad_weight, grad_bias = layer(
        features,
        adjacency.reshape(SLOTS, 256, 256),
        tile_coords.reshape(2, 2, 40),
        tile_counts.reshape(1, 2),
        weight,
        bias.reshape(1, 256),
        cotangent,
        scale,
    )
    hidden, grad_inputs, grad_weight, grad_bias = finish(
        hidden, grad_inputs, grad_weight, grad_bias
    )
    return hidden, grad_inputs[None], grad_weight.reshape(128, 256), grad_bias.reshape(256)


def solution(mesh):
    return jax.shard_map(
        shards,
        mesh=mesh,
        in_specs=(
            P("rows", None),
            P("rows", "rep", None, None, None, None),
            P("rows", "rep", None, None, None),
            P("rows", "rep", None),
            P(),
            P(),
            P(("rows", "rep"), None),
        ),
        out_specs=(P(("rows", "rep"), None), P("rep", None, "rows", None), P(), P()),
        check_vma=False,
    )
```

```python
import functools
import math

import jax
import jax.numpy as jnp
from jax import lax
from jax.experimental import pallas as pl
from jax.experimental.pallas import tpu as pltpu
from jax.sharding import PartitionSpec as P

MESH = pl.DeviceIdType.MESH
F32 = jnp.float32
BF16 = jnp.bfloat16
SLOTS = 80
CHUNKS = (4, 1)
KEEP = (32, 16)
VMEM_BYTES = 62 * 2**20
XY_ORDER = (1, 3, 4, 5, 7, 2, 6)


def mm(a, b):
    return lax.dot_general(a, b, (((1,), (0,)), ((), ())), preferred_element_type=F32)


def mm_nt(a, b):
    return lax.dot_general(a, b, (((1,), (1,)), ((), ())), preferred_element_type=F32)


def mm_tn(a, b):
    return lax.dot_general(a, b, (((0,), (0,)), ((), ())), preferred_element_type=F32)


def arrived(ref, sem):
    pltpu.make_async_copy(ref, ref, sem).wait()


def kernel(
    scale,
    feat_hbm, adj_hbm, coord_hbm, count_hbm, w_hbm, b_hbm, cot_hbm,
    hid_hbm, gin_hbm, gw_hbm, gb_hbm,
    coord, count, place, line, tab, adj, feat, acc, pf, ps, pr, rt, acct, xs0, xs1, xr0, xr1, xa, zs, zr, zf, yf, yr,
    w_ref, b_ref, cot_ref, hid_ref, gin_ref, gw_ref, gb_ref, wa_s, wa, wb, wc,
    adj_sem, in_sem, tab_sem, out_sem, s1, s2, s3, r12, r3, ps_s, ps_r, rt_s, rt_r,
    wa_ss, wa_rs, wb_ss, wb_rs, wc_ss, wc_rs,
    xs_s, xs_r, zs_s, zs_r,
    zf_s, zf_r, yf_s, yf_r,
):
    row = lax.axis_index("rows")
    rep = lax.axis_index("rep")
    x = lax.rem(row, 4)
    z = lax.rem(lax.div(row, 4), 8)
    yl = lax.div(row, 32)
    yh = lax.div(rep, 2)
    core = lax.rem(rep, 2)

    def device(x, yl, z, yh, core):
        return (yl * 32 + z * 4 + x, yh * 2 + core)

    def xy_at(k, sign=1):
        return lax.rem(x + sign * (k % 4) + 4, 4), lax.rem(yl + k // 4, 2)

    def xy_peer(k):
        px, pyl = xy_at(k)
        return device(px, pyl, z, yh, core)

    def z_peer(k):
        return device(x, yl, lax.rem(z + k, 8), yh, core)

    def rep_peer(k):
        return device(x, yl, z, lax.rem(yh + k // 2, 2), lax.rem(core + k % 2, 2))

    a_pos = (yh * 2 + yl) * 4 + x
    b_pos = z * 2 + core

    def a_at(k):
        return lax.rem(a_pos + k, 16)

    def a_peer(k):
        pos = a_at(k)
        py = lax.div(pos, 4)
        return device(lax.rem(pos, 4), lax.rem(py, 2), z, lax.div(py, 2), core)

    def b_peer(k):
        pos = lax.rem(b_pos + k, 16)
        return device(x, yl, lax.div(pos, 2), yh, lax.rem(pos, 2))

    def send(src, dst, send_sem, recv_sem, peer):
        return pltpu.make_async_remote_copy(
            src_ref=src, dst_ref=dst, send_sem=send_sem, recv_sem=recv_sem,
            device_id=peer, device_id_type=MESH,
        )

    sent = []

    barrier = pltpu.get_barrier_semaphore()
    greet = [a_peer(k) for k in range(1, 16)]
    greet += [b_peer(k) for k in range(1, 16)]
    for peer in greet:
        pl.semaphore_signal(barrier, inc=1, device_id=peer, device_id_type=MESH)
    part = SLOTS // 4
    for i in range(4):
        pltpu.make_async_copy(
            adj_hbm.at[pl.ds(i * part, part)], adj.at[pl.ds(i * part, part)], adj_sem.at[i]
        ).start()

    small = [(coord_hbm, coord), (count_hbm, count), (w_hbm, w_ref), (b_hbm, b_ref), (cot_hbm, cot_ref)]
    for i, (src, dst) in enumerate(small):
        pltpu.make_async_copy(src, dst, in_sem.at[i]).start()

    pl.semaphore_wait(barrier, len(greet))

    my_j = yl * 4 + x
    is_root = [row == (rep * 2 + s) * 8 for s in range(2)]
    in_plane = [z == core * 4 + s * 2 for s in range(2)]

    def span(s, c):
        size = 256 // CHUNKS[s]
        return pl.ds(c * size, size)

    def root_copy(s, c, k):
        px, pyl = xy_at(k)
        j = pyl * 4 + px
        size = 256 // CHUNKS[s]
        return send(
            feat_hbm.at[pl.ds(pl.multiple_of(j * 256 + c * size, size), size)], feat.at[s, j, span(s, c)],
            s1.at[s, c, k], r12.at[s, c], device(px, pyl, z, yh, core),
        )

    def plane_copy(s, c, k):
        mine = feat.at[s, my_j, span(s, c)]
        return send(mine, mine, s2.at[s, c, k], r12.at[s, c], z_peer(k))

    def side_copy(s, c, k):
        mine = feat.at[s, my_j, span(s, c)]
        return send(mine, mine, s3.at[s, c, k], r3.at[s, c, k], xy_peer(k))

    def drain_if(cond, copy, s):
        @pl.when(cond)
        def _():
            for c in range(CHUNKS[s]):
                for k in range(1, 8):
                    copy(s, c, k).wait_send()

    for s in range(2):
        @pl.when(is_root[s])
        def _():
            for c in range(CHUNKS[s]):
                size = 256 // CHUNKS[s]
                for k in XY_ORDER:
                    root_copy(s, c, k).start()
                pltpu.make_async_copy(
                    feat_hbm.at[pl.ds(pl.multiple_of(my_j * 256 + c * size, size), size)],
                    feat.at[s, my_j, span(s, c)], r12.at[s, c],
                ).start()

        sent.append(functools.partial(drain_if, is_root[s], root_copy, s))

    acc[...] = jnp.zeros_like(acc)
    adj[SLOTS] = jnp.zeros((256, 256), BF16)

    for i, (src, dst) in enumerate(small):
        arrived(dst, in_sem.at[i])
    place[...] = jnp.full((8, 128), -1, jnp.int32)
    slot = lax.broadcasted_iota(jnp.int32, (1, 40), 1)
    for s in range(2):
        where = coord[s, pl.ds(0, 1)] * 8 + coord[s, pl.ds(1, 1)] + s * 64
        place[pl.ds(s, 1), pl.ds(0, 40)] = jnp.where(slot < count[:, s : s + 1], where, -1)
    by_slot = place[...].T
    spot = lax.broadcasted_iota(jnp.int32, (128, 128), 1)
    number = lax.broadcasted_iota(jnp.int32, (128, 128), 0) - SLOTS
    found = jnp.where(by_slot[:, 0:1] == spot, number, 0)
    found += jnp.where(by_slot[:, 1:2] == spot, number + 40, 0)
    line[...] = jnp.sum(found, axis=0, keepdims=True) + SLOTS
    to_scalar = pltpu.make_async_copy(line, tab, tab_sem)
    to_scalar.start()
    to_scalar.wait()

    for s in range(2):
        @pl.when(in_plane[s])
        def _():
            for c in range(CHUNKS[s]):
                arrived(feat.at[s, my_j, span(s, c)], r12.at[s, c])
                for k in (4, 3, 5, 2, 6, 1, 7):
                    plane_copy(s, c, k).start()

        sent.append(functools.partial(drain_if, in_plane[s], plane_copy, s))

    for s in range(2):
        for c in range(CHUNKS[s]):
            @pl.when(jnp.logical_not(in_plane[s]))
            def _():
                arrived(feat.at[s, my_j, span(s, c)], r12.at[s, c])

            for k in XY_ORDER:
                side_copy(s, c, k).start()
                sent.append(side_copy(s, c, k).wait_send)

    for i in range(4):
        view = adj.at[pl.ds(i * part, part)]
        arrived(view, adj_sem.at[i])

    def landed(s, k):
        fx = lax.rem(x - lax.rem(k, 4) + 4, 4)
        fyl = lax.rem(yl + lax.div(k, 4), 2)
        j = fyl * 4 + fx

        @pl.when(k > 0)
        def _():
            for c in range(CHUNKS[s]):
                arrived(feat.at[s, j, span(s, c)], r3.at[s, c, k])

        return j, feat[s, j]

    def forward(s, k, carry):
        j, column = landed(s, k)
        for p in range(8):
            acc[p] += mm(adj[tab[0, s * 64 + p * 8 + j]], column)
        return carry

    for s in range(2):
        lax.fori_loop(0, 8 - 2 * s, functools.partial(forward, s), 0, unroll=2)
    forward(1, 6, 0)
    last, column = landed(1, 7)

    def last_term(p):
        acc[p] += mm(adj[tab[0, 64 + p * 8 + last]], column)

    far_yh, other = lax.rem(yh + 1, 2), lax.rem(core + 1, 2)

    def core_copy(i):
        quarter = (far_yh, yh)[i // 2] * 2 + other
        return send(acc.at[quarter * 2 + i % 2], pf.at[i // 2, i % 2], ps_s.at[i], ps_r.at[i], rep_peer(1))

    def far_copy(h):
        return send(ps.at[h], pr.at[h], ps_s.at[4 + h], ps_r.at[4 + h], rep_peer(2))

    for i in range(4):
        last_term(((far_yh, yh)[i // 2] * 2 + other) * 2 + i % 2)
        core_copy(i).start()
        sent.append(core_copy(i).wait_send)
    for i in range(4):
        last_term(((far_yh, yh)[i // 2] * 2 + core) * 2 + i % 2)
    for h in range(2):
        arrived(pf.at[0, h], ps_r.at[h])
        ps[h] = (acc[(far_yh * 2 + core) * 2 + h] + pf[0, h]).astype(BF16)
        far_copy(h).start()
        sent.append(far_copy(h).wait_send)
    for h in range(2):
        arrived(pf.at[1, h], ps_r.at[2 + h])

    c0 = math.sqrt(2.0 / math.pi)
    weight = w_ref[...]

    def far_rows(h):
        return send(rt.at[rep, h], rt.at[rep, h], rt_s.at[h], rt_r.at[h], rep_peer(2))

    def pass_on(h):
        far = rt.at[lax.rem(yh + 1, 2) * 2 + core, h]
        return send(far, far, rt_s.at[2 + h], rt_r.at[2 + h], rep_peer(1))

    def near_rows():
        return send(rt.at[rep], rt.at[rep], rt_s.at[4], rt_r.at[4], rep_peer(1))

    def epilogue(h, carry):
        wsum, bsum = carry
        rows = pl.ds(pl.multiple_of(h * 256, 256), 256)
        total = acc[rep * 2 + h] + pf[1, h]
        arrived(pr.at[h], ps_r.at[4 + h])
        total += pr[h].astype(F32)
        agg = total.astype(BF16)
        v = mm(agg, weight) + b_ref[...]
        v2 = v * v
        t = jnp.tanh(c0 * (v + 0.044715 * (v2 * v)))
        half = 0.5 * (1.0 + t)
        hid_ref[rows] = (v * half).astype(BF16)
        slope = half + 0.5 * v * (1.0 - t * t) * (c0 * (1.0 + 0.134145 * v2))
        grad = cot_ref[rows].astype(F32) * slope
        grad_bf = grad.astype(BF16)
        rt[rep, h] = mm_nt(weight, grad_bf).astype(BF16)
        far_rows(h).start()
        sent.append(far_rows(h).wait_send)
        wsum = wsum + mm_tn(agg, grad_bf)
        bsum = bsum + jnp.sum(grad.reshape(32, 8, 256), axis=0)
        return wsum, bsum

    carry = (jnp.zeros((128, 256), F32), jnp.zeros((8, 256), F32))
    for h in range(2):
        carry = epilogue(h, carry)
    wsum, bsum = carry

    def put(i, src, dst):
        copy = pltpu.make_async_copy(src, dst, out_sem.at[i])
        copy.start()
        sent.append(copy.wait)

    near_rows().start()
    sent.append(near_rows().wait_send)

    put(0, hid_ref, hid_hbm)

    for j in range(16):
        for h in range(2):
            wa_s[j, pl.ds(h * 8, 8)] = wsum[j * 8 : j * 8 + 8, h * 128 : h * 128 + 128]
        wa_s[j, pl.ds(16, 8)] = bsum[:, (j % 2) * 128 : (j % 2) * 128 + 128]

    def wa_copy(k):
        return send(wa_s.at[a_at(k)], wa.at[a_pos], wa_ss.at[k], wa_rs.at[k], a_peer(k))

    for k in range(1, 16):
        wa_copy(k).start()
        sent.append(wa_copy(k).wait_send)
    wa[a_pos] = wa_s[a_pos]

    def wb_copy(k):
        return send(wb.at[b_pos], wb.at[b_pos], wb_ss.at[k], wb_rs.at[k], b_peer(k))

    def add_up(ref):
        total = ref[0]
        for j in range(1, 16):
            total = total + ref[j]
        return total

    def step_b():
        for k in range(1, 16):
            arrived(wa.at[lax.rem(a_pos - k + 16, 16)], wa_rs.at[k])
        wb[b_pos] = add_up(wa)
        for k in range(1, 16):
            wb_copy(k).start()
            sent.append(wb_copy(k).wait_send)

    def wc_copy(k):
        return send(wc.at[a_pos], wc.at[a_pos], wc_ss.at[k], wc_rs.at[k], a_peer(k))

    def step_c():
        for k in range(1, 16):
            arrived(wb.at[lax.rem(b_pos - k + 16, 16)], wb_rs.at[k])
        wc[a_pos] = add_up(wb) * scale
        for k in range(1, 16):
            wc_copy(k).start()
            sent.append(wc_copy(k).wait_send)

    def quarter_of(k):
        return lax.rem(yh + k // 2, 2) * 2 + lax.rem(core + k % 2, 2)

    def back_term(s, q, quarter, h):
        return mm(rt[quarter, h], adj[tab[0, s * 64 + quarter * 16 + h * 8 + q]])

    def back_terms(s, q, quarter):
        return back_term(s, q, quarter, 0) + back_term(s, q, quarter, 1)

    def back_own(i, carry):
        s, q = lax.div(i, 8), lax.rem(i, 8)
        acct[s, q] = back_terms(s, q, quarter_of(0))
        return carry

    lax.fori_loop(0, 16, back_own, 0, unroll=4)
    arrived(rt.at[quarter_of(1)], rt_r.at[4])

    def back_core(i, carry):
        s, q = lax.div(i, 8), lax.rem(i, 8)
        acct[s, q] += back_terms(s, q, quarter_of(1))
        return carry

    lax.fori_loop(0, 16, back_core, 0, unroll=4)
    def back_far(h, i, carry):
        s, q = lax.div(i, 8), lax.rem(i, 8)
        acct[s, q] += back_term(s, q, quarter_of(2), h)
        return carry

    for h in range(2):
        arrived(rt.at[quarter_of(2), h], rt_r.at[h])
        pass_on(h).start()
        sent.append(pass_on(h).wait_send)
        if h == 1:
            step_b()
        lax.fori_loop(0, 16, functools.partial(back_far, h), 0, unroll=4)
    for h in range(2):
        arrived(rt.at[quarter_of(3), h], rt_r.at[2 + h])

    xs, xr = (xs0, xs1), (xr0, xr1)

    def xs_copy(s, k):
        px, pyl = xy_at(k)
        return send(xs[s].at[pyl * 4 + px], xr[s].at[k], xs_s.at[s, k], xs_r.at[s, k], xy_peer(k))

    late = pl.ds(KEEP[1], 32 - KEEP[1])

    def zf_copy(k):
        return send(xa.at[lax.rem(z + k, 8)], zf.at[k], zf_s.at[k], zf_r.at[k], z_peer(k))

    def yf_copy(k):
        px, pyl = xy_at(k)
        return send(yf.at[pyl * 4 + px], yr.at[k], yf_s.at[k], yf_r.at[k], xy_peer(k))

    for s in range(2):
        for hk in (1, 0):
            half = lax.rem(yl + hk, 2)

            def back_rest(zz, carry):
                q = half * 4 + zz
                total = acct[s, q] + back_terms(s, q, quarter_of(3))
                out = total.T.astype(BF16)
                for zl in range(2):
                    for px in range(4):
                        at = zl * 128 + px * 32
                        keep = KEEP[s]
                        xs[s][half * 4 + px, zz * 2 + zl] = out[at : at + keep]
                        if s == 1:
                            xa[zz * 2 + zl, half * 4 + px] = out[at + keep : at + 32]
                return carry

            lax.fori_loop(0, 4, back_rest, 0, unroll=True)
            for k in (1, 3, 2) if hk == 0 else (4, 5, 7, 6):
                xs_copy(s, k).start()
                sent.append(xs_copy(s, k).wait_send)
    for k in (4, 3, 5, 2, 6, 1, 7):
        zf_copy(k).start()
        sent.append(zf_copy(k).wait_send)

    step_c()

    def zs_copy(s, k):
        rows = pl.ds(0, KEEP[s])
        return send(
            zs.at[s, lax.rem(z + k, 8), rows], zr.at[s, k, rows], zs_s.at[s, k], zs_r.at[s, k], z_peer(k)
        )

    def over_xy(s):
        rows = pl.ds(0, KEEP[s])
        for k in range(1, 8):
            arrived(xr[s].at[k], xs_r.at[s, k])
        for zz in range(8):
            total = xs[s][my_j, zz].astype(F32)
            for k in range(1, 8):
                total += xr[s][k, zz].astype(F32)
            zs[s, zz, rows] = total.astype(BF16)
        for k in (4, 3, 5, 2, 6, 1, 7):
            zs_copy(s, k).start()
            sent.append(zs_copy(s, k).wait_send)

    over_xy(0)
    for k in range(1, 8):
        arrived(zf.at[k], zf_r.at[k])
    for j in range(8):
        total = xa[z, j].astype(F32)
        for k in range(1, 8):
            total += zf[k, j].astype(F32)
        yf[j] = total.astype(BF16)
    for k in XY_ORDER:
        yf_copy(k).start()
        sent.append(yf_copy(k).wait_send)
    over_xy(1)

    for s in range(2):
        rows = pl.ds(0, KEEP[s])
        total = zs[s, z, rows].astype(F32)
        for k in range(1, 8):
            arrived(zr.at[s, k, rows], zs_r.at[s, k])
            total += zr[s, k, rows].astype(F32)
        gin_ref[s, rows] = total.astype(BF16)
    total = yf[my_j].astype(F32)
    for k in range(1, 8):
        arrived(yr.at[k], yf_r.at[k])
        total += yr[k].astype(F32)
    gin_ref[1, late] = total.astype(BF16)
    put(1, gin_ref, gin_hbm)

    for k in range(1, 16):
        arrived(wc.at[lax.rem(a_pos - k + 16, 16)], wc_rs.at[k])
    for j in range(16):
        for h in range(2):
            gw_ref[j, :, pl.ds(h * 128, 128)] = wc[j, pl.ds(h * 8, 8)]
    for h in range(2):
        gb_ref[:, pl.ds(h * 128, 128)] = jnp.sum(wc[h, pl.ds(16, 8)], axis=0, keepdims=True)
    put(2, gw_ref, gw_hbm)
    put(3, gb_ref, gb_hbm)

    for drain in sent:
        drain()


def layer(features, adjacency, coords, counts, weight, bias, cotangent, scale):
    hbm = pl.BlockSpec(memory_space=pltpu.HBM)
    sems = [
        (4,), (5,), (), (4,), (2, 4, 8), (2, 4, 8), (2, 4, 8), (2, 4), (2, 4, 8), (8,), (8,), (8,), (8,),
        (16,), (16,), (16,), (16,), (16,), (16,),
        (2, 8), (2, 8), (2, 8), (2, 8), (8,), (8,), (8,), (8,),
    ]
    return pl.pallas_call(
        functools.partial(kernel, scale),
        name="layer",
        out_shape=(
            jax.ShapeDtypeStruct((512, 256), BF16),
            jax.ShapeDtypeStruct((2, 32, 128), BF16),
            jax.ShapeDtypeStruct((16, 8, 256), F32),
            jax.ShapeDtypeStruct((1, 256), F32),
        ),
        in_specs=[hbm] * 7,
        out_specs=(hbm, hbm, hbm, hbm),
        scratch_shapes=[
            pltpu.VMEM((2, 2, 40), jnp.int32),
            pltpu.VMEM((1, 2), jnp.int32),
            pltpu.VMEM((8, 128), jnp.int32),
            pltpu.VMEM((1, 128), jnp.int32),
            pltpu.SMEM((1, 128), jnp.int32),
            pltpu.VMEM((SLOTS + 1, 256, 256), BF16),
            pltpu.VMEM((2, 8, 256, 128), BF16),
            pltpu.VMEM((8, 256, 128), F32),
            pltpu.VMEM((2, 2, 256, 128), F32),
            pltpu.VMEM((2, 256, 128), BF16),
            pltpu.VMEM((2, 256, 128), BF16),
            pltpu.VMEM((4, 2, 128, 256), BF16),
            pltpu.VMEM((2, 8, 128, 256), F32),
            pltpu.VMEM((8, 8, KEEP[0], 128), BF16),
            pltpu.VMEM((8, 8, KEEP[1], 128), BF16),
            pltpu.VMEM((8, 8, KEEP[0], 128), BF16),
            pltpu.VMEM((8, 8, KEEP[1], 128), BF16),
            pltpu.VMEM((8, 8, 32 - KEEP[1], 128), BF16),
            pltpu.VMEM((2, 8, 32, 128), BF16),
            pltpu.VMEM((2, 8, 32, 128), BF16),
            pltpu.VMEM((8, 8, 16, 128), BF16),
            pltpu.VMEM((8, 16, 128), BF16),
            pltpu.VMEM((8, 16, 128), BF16),
            pltpu.VMEM((128, 256), BF16),
            pltpu.VMEM((1, 256), F32),
            pltpu.VMEM((512, 256), BF16),
            pltpu.VMEM((512, 256), BF16),
            pltpu.VMEM((2, 32, 128), BF16),
            pltpu.VMEM((16, 8, 256), F32),
            pltpu.VMEM((1, 256), F32),
            pltpu.VMEM((16, 24, 128), F32),
            pltpu.VMEM((16, 24, 128), F32),
            pltpu.VMEM((16, 24, 128), F32),
            pltpu.VMEM((16, 24, 128), F32),
        ]
        + [pltpu.SemaphoreType.DMA(shape) for shape in sems],
        compiler_params=pltpu.CompilerParams(
            collective_id=1, has_side_effects=True, vmem_limit_bytes=VMEM_BYTES
        ),
    )(features, adjacency, coords, counts, weight, bias, cotangent)


def finish_kernel(n, *refs):
    ins, outs, held, sem = refs[:n], refs[n : 2 * n], refs[2 * n : 3 * n], refs[3 * n]
    loads = [pltpu.make_async_copy(ins[i], held[i], sem.at[0, i]) for i in range(n)]
    stores = [pltpu.make_async_copy(held[i], outs[i], sem.at[1, i]) for i in range(n)]
    for copy in loads:
        copy.start()
    for load, store in zip(loads, stores):
        load.wait()
        store.start()
    for copy in stores:
        copy.wait()


def finish(*arrays):
    n = len(arrays)
    hbm = pl.BlockSpec(memory_space=pltpu.HBM)
    return pl.pallas_call(
        functools.partial(finish_kernel, n),
        name="finish",
        out_shape=tuple(jax.ShapeDtypeStruct(a.shape, a.dtype) for a in arrays),
        in_specs=[hbm] * n,
        out_specs=(hbm,) * n,
        scratch_shapes=[pltpu.VMEM(a.shape, a.dtype) for a in arrays]
        + [pltpu.SemaphoreType.DMA((2, n))],
        compiler_params=pltpu.CompilerParams(vmem_limit_bytes=VMEM_BYTES),
    )(*arrays)


def shards(features, adjacency, tile_coords, tile_counts, weight, bias, cotangent):
    rows_count = lax.axis_size("rows")
    scale = 1.0 / math.sqrt(features.shape[0] * rows_count)
    hidden, grad_inputs, grad_weight, grad_bias = layer(
        features,
        adjacency.reshape(SLOTS, 256, 256),
        tile_coords.reshape(2, 2, 40),
        tile_counts.reshape(1, 2),
        weight,
        bias.reshape(1, 256),
        cotangent,
        scale,
    )
    hidden, grad_inputs, grad_weight, grad_bias = finish(
        hidden, grad_inputs, grad_weight, grad_bias
    )
    return hidden, grad_inputs[None], grad_weight.reshape(128, 256), grad_bias.reshape(256)


def solution(mesh):
    return jax.shard_map(
        shards,
        mesh=mesh,
        in_specs=(
            P("rows", None),
            P("rows", "rep", None, None, None, None),
            P("rows", "rep", None, None, None),
            P("rows", "rep", None),
            P(),
            P(),
            P(("rows", "rep"), None),
        ),
        out_specs=(P(("rows", "rep"), None), P("rep", None, "rows", None), P(), P()),
        check_vma=False,
    )
```
